512 devices in a mesh: pipe: 16 (over x_lo, y, core), expert: 32 (over z, x_hi).
Axes of the slice: x: 4 (x_hi: 2, x_lo: 2; x = x_hi * 2 + x_lo), y: 4, z: 16, core: 2. Of those that a mesh axis runs over, the one named last changes fastest.
Arguments:
- fwd_tokens: bfloat16 [16, 256, 3584], P('pipe', 'expert'), may hold values from -6 to 6
- saved_tokens: bfloat16 [2, 16, 256, 3584], P(None, 'pipe', 'expert'), may hold values from -6 to 6
- cotangent: bfloat16 [16, 256, 3584], P('pipe', 'expert'), may hold values from -6 to 6
- fwd_routes: int32 [2, 16, 256, 2], P(None, 'pipe', 'expert'), may hold values from 0 to 3, all different within a row; in each aligned block of 8 rows (0 to 7, 8 to 15, ..., all dimensions but the last counted through in order) at most 5 rows name the same one
- bwd_routes: int32 [2, 16, 256, 2], P(None, 'pipe', 'expert'), may hold values from 0 to 3, all different within a row; in each aligned block of 8 rows (0 to 7, 8 to 15, ..., all dimensions but the last counted through in order) at most 5 rows name the same one
- norm_gain: float32 [16, 3584], P('pipe'), may hold values from 0.1 to 1.9
- router: bfloat16 [16, 3584, 4], P('pipe'), may hold values from -0.09375 to 0.09375
- w_gate: bfloat16 [16, 3584, 4096], P('pipe', None, 'expert'), may hold values from -0.09375 to 0.09375
- w_up: bfloat16 [16, 3584, 4096], P('pipe', None, 'expert'), may hold values from -0.09375 to 0.09375
- w_down: bfloat16 [16, 4096, 3584], P('pipe', 'expert'), may hold values from -0.1875 to 0.1875
Outputs:
- fwd_out: bfloat16 [16, 256, 3584], P('pipe', 'expert')
- bwd_out: bfloat16 [16, 256, 3584], P('pipe', 'expert')
The draws below stay inside these ranges and needn't reach their ends.
Inputs may be any that keep to these rules, and one draw needn't show every extreme that they name: `fwd_routes`: each row names 2 different experts. In every aligned block of 8 rows (one device's tokens of one step and section) no expert is named more than 5 times; in at least one block some expert is named exactly 5 times. `bwd_routes`: each row names 2 different experts. In every aligned block of 8 rows (one device's tokens of one step and section) no expert is named more than 5 times; in at least one block some expert is named exactly 5 times.
All inputs are finite; a program needn't handle non-finite values.
Results may differ from the reference program's by a relative error of at most 0.018.
Values may be sent and summed in bfloat16 or wider, within the bound.
No kernel may reach another device: no remote copies, remote signals or barrier semaphores. Data moves between devices by JAX's collectives and lax.ppermute only.
A program may use at most 64 MiB of HBM per device.

```python
import math
import jax
import jax.numpy as jnp
import numpy as np
from jax import lax

D = 3584
FFE = 1024
TOP = 2
EXPERTS = 4
TICKS = 2
TOK_DEV = 8
CAP = 5
TOKENS = 256
SECTIONS = 16
N_EXPERT = 32


def level_of(key, extent, shards, smallest, top_value):
    def one(dim, shards_of):
        steps = jax.random.uniform(jax.random.fold_in(jax.random.fold_in(key, 6), dim), (shards_of,), jnp.float32, smallest / len(shards), top_value / len(shards))
        return jnp.repeat(jnp.exp(steps), extent[dim] // shards_of).reshape((-1,) + (1,) * (len(extent) - dim - 1))

    factor_of = one(*shards[0])
    for cut in shards[1:]:
        factor_of = factor_of * one(*cut)
    return factor_of


def shared_out(own_key, own, number, rows, number_of, top, bound, slope):
    sequence = jax.random.permutation(own_key, number_of)
    crowded, usual = portions_of(number_of, rows * top, bound, slope, True), portions_of(number_of, rows * top, bound, slope, False)
    places = jnp.arange(number_of)

    def named(lengths, offset_by):
        used = int((lengths > 0).sum())
        fixed = max(1, used // 4)
        shifted = fixed + (places - fixed + offset_by * (used - fixed)) % max(1, number_of - fixed)
        return jnp.zeros((number_of,), jnp.int32).at[sequence[jnp.where(places < fixed, places, shifted)]].set(jnp.asarray(lengths, jnp.int32))

    lengths = jnp.where(number % 4 == 0, named(crowded, number // 4), named(usual, number - number // 4 - 1))
    mixed = jax.random.permutation(jax.random.fold_in(own, 3), number_of)
    source_of, taker = mixed[0:number_of // 2 * 2:2], mixed[1:number_of // 2 * 2:2]
    slack = jnp.minimum(lengths[source_of] - 1, bound - lengths[taker]) // 2
    slack = jnp.where((source_of == sequence[0]) | (taker == sequence[0]) | (lengths[taker] == 0), 0, jnp.maximum(slack, 0))
    shifted = jax.random.randint(jax.random.fold_in(own, 4), (number_of // 2,), 0, 1 << 20) % (slack + 1)
    lengths = lengths.at[source_of].add(-shifted).at[taker].add(shifted)
    items = jnp.searchsorted(jnp.cumsum(lengths), jnp.arange(rows * top), side="right").astype(jnp.int32)
    listing = items.reshape(top, rows).T
    listing = listing[jax.random.permutation(jax.random.fold_in(own, 1), rows)]
    offset_by = jax.random.randint(jax.random.fold_in(own, 2), (rows, 1), 0, top)
    return jnp.take_along_axis(listing, (jnp.arange(top)[None, :] + offset_by) % top, axis=1)


def portions_of(count, total, most, slope, full):
    weights = [(1 << 20) // math.isqrt(standing ** slope) + 1 for standing in range(1, count + 1)]
    largest = most if full else min(most, max(-(-total // count), total * weights[0] // sum(weights)))
    least = 1 if total - largest >= count - 1 else 0
    holding, surplus = [largest] + [least] * (count - 1), total - largest - least * (count - 1)
    while surplus > 0:
        free = [i for i in range(1, count) if holding[i] < largest] or [i for i in range(1, count) if holding[i] < most]
        whole, remaining = sum([weights[i] for i in free]), surplus
        for i in free:
            more = min(most - holding[i], max(1, remaining * weights[i] // whole), surplus)
            holding[i] = holding[i] + more
            surplus = surplus - more
    return np.array(holding)


def normal_values(rng, shape, width, reach, pieces=(), kind=jnp.bfloat16):
    level = level_of(rng, shape, pieces, -0.22, 0.18) if pieces else 1.0
    values = jax.random.normal(rng, shape, jnp.float32) * width * level
    return jnp.minimum(jnp.maximum(values, -reach), reach).astype(kind)


def setup_inputs(seed: int = 0) -> dict:
    streams_of = jax.random.split(jax.random.key(seed), 11)
    fwd_tokens = normal_values(streams_of[0], (SECTIONS, TOKENS, D), 1.0, 6.0, ((0, 16), (1, 32)))
    saved_tokens = normal_values(streams_of[1], (TICKS, SECTIONS, TOKENS, D), 1.0, 6.0, ((1, 16), (2, 32)))
    cotangent = normal_values(streams_of[2], (SECTIONS, TOKENS, D), 1.0, 6.0, ((0, 16), (1, 32)))
    fwd_routes_keys = jax.random.split(jax.random.fold_in(streams_of[3], 1), TICKS * SECTIONS * TOKENS // TOK_DEV)
    fwd_routes_turns = jax.random.permutation(jax.random.fold_in(streams_of[3], 3), TICKS * SECTIONS * TOKENS // TOK_DEV)
    fwd_routes = jax.vmap(lambda own, number: shared_out(jax.random.fold_in(streams_of[3], 2), own, number, TOK_DEV, EXPERTS, TOP, CAP, 1))(fwd_routes_keys, fwd_routes_turns).reshape((TICKS, SECTIONS, TOKENS, TOP))
    bwd_routes_keys = jax.random.split(jax.random.fold_in(streams_of[4], 1), TICKS * SECTIONS * TOKENS // TOK_DEV)
    bwd_routes_turns = jax.random.permutation(jax.random.fold_in(streams_of[4], 3), TICKS * SECTIONS * TOKENS // TOK_DEV)
    bwd_routes = jax.vmap(lambda own, number: shared_out(jax.random.fold_in(streams_of[4], 2), own, number, TOK_DEV, EXPERTS, TOP, CAP, 1))(bwd_routes_keys, bwd_routes_turns).reshape((TICKS, SECTIONS, TOKENS, TOP))
    norm_gain = jnp.clip(1.0 + 0.18 * jax.random.normal(streams_of[5], (SECTIONS, D), jnp.float32), 0.1, 1.9)
    router = normal_values(streams_of[6], (SECTIONS, D, EXPERTS), D ** -0.5, 0.09375, ((0, 16),))
    w_gate = normal_values(streams_of[7], (SECTIONS, D, EXPERTS * FFE), D ** -0.5, 0.09375, ((0, 16), (2, 32)))
    w_up = normal_values(streams_of[8], (SECTIONS, D, EXPERTS * FFE), D ** -0.5, 0.09375, ((0, 16), (2, 32)))
    w_down = normal_values(streams_of[9], (SECTIONS, EXPERTS * FFE, D), FFE ** -0.5, 0.1875, ((0, 16), (1, 32)))
    return {"fwd_tokens": fwd_tokens, "saved_tokens": saved_tokens, "cotangent": cotangent, "fwd_routes": fwd_routes, "bwd_routes": bwd_routes, "norm_gain": norm_gain, "router": router, "w_gate": w_gate, "w_up": w_up, "w_down": w_down}


def norm_rows(values, norm_gain):
    wide = values.astype(jnp.float32)
    scale = lax.rsqrt(lax.optimization_barrier(jnp.mean(wide * wide, axis=-1, keepdims=True)) + 1e-06)
    return wide * scale * norm_gain.astype(jnp.float32)

def gate_values(normed, router_w, routes, expert_count):
    logits = jnp.dot(normed, router_w, preferred_element_type=jnp.float32)
    sig_all = jax.nn.sigmoid(logits)
    route_pick = (routes[..., None] == jnp.arange(expert_count, dtype=jnp.int32)).astype(jnp.float32)
    chosen = lax.optimization_barrier(jnp.sum(route_pick * sig_all[:, None, :], axis=-1))
    gate_total = lax.optimization_barrier(jnp.sum(chosen, axis=-1, keepdims=True))
    gate_share = chosen / gate_total
    return (chosen, gate_total, gate_share, route_pick)

def slot_matrix(routes, expert_count, cap_rows):
    flat_routes = routes.reshape(-1).astype(jnp.int32)
    hit_table = (flat_routes[:, None] == jnp.arange(expert_count, dtype=jnp.int32)).astype(jnp.int32)
    before = jnp.cumsum(hit_table, axis=0) - hit_table
    slot_index = lax.optimization_barrier(jnp.sum(before * hit_table, axis=1))
    position = flat_routes * cap_rows + slot_index
    placement = (position[:, None] == jnp.arange(expert_count * cap_rows, dtype=jnp.int32)).astype(jnp.float32)
    return placement.reshape(routes.shape[0], routes.shape[1], expert_count * cap_rows)

def expert_forward(row_block, gate_w, up_w, down_w):
    gate_pre = jnp.dot(row_block, gate_w, preferred_element_type=jnp.float32)
    up_pre = jnp.dot(row_block, up_w, preferred_element_type=jnp.float32)
    hidden = (jax.nn.silu(gate_pre) * up_pre).astype(jnp.bfloat16)
    return jnp.dot(hidden, down_w, preferred_element_type=jnp.float32).astype(jnp.bfloat16)

def expert_backward(row_block, cotan_rows, gate_w, up_w, down_w):
    gate_pre = jnp.dot(row_block, gate_w, preferred_element_type=jnp.float32)
    up_pre = jnp.dot(row_block, up_w, preferred_element_type=jnp.float32)
    gate_sig = jax.nn.sigmoid(gate_pre)
    gate_act = gate_pre * gate_sig
    hidden = (gate_act * up_pre).astype(jnp.bfloat16)
    expert_out = jnp.dot(hidden, down_w, preferred_element_type=jnp.float32).astype(jnp.bfloat16)
    hidden_grad = jnp.einsum('rd,fd->rf', cotan_rows, down_w, preferred_element_type=jnp.float32)
    gate_grad = (hidden_grad * up_pre * gate_sig * (1.0 + gate_pre * (1.0 - gate_sig))).astype(jnp.bfloat16)
    up_grad = (hidden_grad * gate_act).astype(jnp.bfloat16)
    row_grad = jnp.einsum('rf,df->rd', gate_grad, gate_w, preferred_element_type=jnp.float32)
    row_grad = row_grad + jnp.einsum('rf,df->rd', up_grad, up_w, preferred_element_type=jnp.float32)
    return (row_grad.astype(jnp.bfloat16), expert_out)

def token_grad(saved, cotan, norm_gain, router_w, chosen, gate_total, gate_share, route_pick, dgate, row_sum):
    dchosen = (dgate - lax.optimization_barrier(jnp.sum(gate_share * dgate, axis=-1, keepdims=True))) / gate_total
    logit_grad = dchosen * chosen * (1.0 - chosen)
    logit_full = jnp.einsum('tk,tke->te', logit_grad, route_pick, precision=lax.Precision.HIGHEST)
    router_back = jnp.dot(logit_full, router_w.astype(jnp.float32).T, precision=lax.Precision.HIGHEST)
    _, norm_pull = jax.vjp(lambda values: norm_rows(values, norm_gain), saved.astype(jnp.float32))
    return (cotan.astype(jnp.float32) + norm_pull(row_sum + router_back)[0]).astype(jnp.bfloat16)

def to_experts(buffer):
    return buffer.reshape(N_EXPERT, EXPERTS, CAP, D).transpose(1, 0, 2, 3).reshape(EXPERTS, N_EXPERT * CAP, D)

def part_weights(gate_w, up_w, down_w):
    split_count = N_EXPERT // EXPERTS
    part_units = FFE // split_count
    gate_parts = gate_w.reshape(D, EXPERTS, split_count, part_units).transpose(1, 2, 0, 3)
    up_parts = up_w.reshape(D, EXPERTS, split_count, part_units).transpose(1, 2, 0, 3)
    down_parts = down_w.reshape(EXPERTS, split_count, part_units, D)
    return (gate_parts, up_parts, down_parts)

def unfold_parts(partial_value):
    split_count = N_EXPERT // EXPERTS
    return partial_value.reshape(EXPERTS, split_count, N_EXPERT, CAP, D).astype(jnp.float32)

def section_step(packed):
    tokens_in, saved, cotan, routes_f, routes_b, norm_gain, router_w, gate_w, up_w, down_w = packed
    gate_parts, up_parts, down_parts = part_weights(gate_w, up_w, down_w)
    normed = norm_rows(tokens_in, norm_gain).astype(jnp.bfloat16)
    chosen_f, total_f, share_f, pick_f = gate_values(normed, router_w, routes_f, EXPERTS)
    gb_f = share_f.astype(jnp.bfloat16).astype(jnp.float32)
    place_f = jax.vmap(lambda block: slot_matrix(block, EXPERTS, CAP))(routes_f.reshape(N_EXPERT, TOK_DEV, TOP))
    spread_f = lax.optimization_barrier(jnp.sum(place_f, axis=2))
    weighted_f = lax.optimization_barrier(jnp.sum(place_f * gb_f.reshape(N_EXPERT, TOK_DEV, TOP, 1), axis=2))
    send_f = jnp.einsum('ntp,ntd->npd', spread_f, normed.astype(jnp.float32).reshape(N_EXPERT, TOK_DEV, D)).astype(jnp.bfloat16)

    def forward_expert(item):
        expert_rows, gate_e, up_e, down_e = item
        return lax.map(lambda part: expert_forward(expert_rows, part[0], part[1], part[2]), (gate_e, up_e, down_e))
    out_f = unfold_parts(lax.map(forward_expert, (to_experts(send_f), gate_parts, up_parts, down_parts)))
    weighted_four = weighted_f.reshape(N_EXPERT, TOK_DEV, EXPERTS, CAP)
    mixture = jnp.einsum('ntec,ejncd->ntd', weighted_four, out_f, precision=lax.Precision.HIGHEST).reshape(TOKENS, D)
    fwd_result = (tokens_in.astype(jnp.float32) + mixture).astype(jnp.bfloat16)
    saved_norm = norm_rows(saved, norm_gain).astype(jnp.bfloat16)
    chosen_b, total_b, share_b, pick_b = gate_values(saved_norm, router_w, routes_b, EXPERTS)
    gb_b = share_b.astype(jnp.bfloat16).astype(jnp.float32)
    place_b = jax.vmap(lambda block: slot_matrix(block, EXPERTS, CAP))(routes_b.reshape(N_EXPERT, TOK_DEV, TOP))
    spread_b = lax.optimization_barrier(jnp.sum(place_b, axis=2))
    weighted_b = lax.optimization_barrier(jnp.sum(place_b * gb_b.reshape(N_EXPERT, TOK_DEV, TOP, 1), axis=2))
    cot_blocks = cotan.astype(jnp.float32).reshape(N_EXPERT, TOK_DEV, D)
    send_m = jnp.einsum('ntp,ntd->npd', spread_b, saved_norm.astype(jnp.float32).reshape(N_EXPERT, TOK_DEV, D)).astype(jnp.bfloat16)
    send_c = jnp.einsum('ntp,ntd->npd', weighted_b, cot_blocks).astype(jnp.bfloat16)

    def backward_expert(item):
        expert_rows, expert_cot, gate_e, up_e, down_e = item
        return lax.map(lambda part: expert_backward(expert_rows, expert_cot, part[0], part[1], part[2]), (gate_e, up_e, down_e))
    grad_e, out_e = lax.map(backward_expert, (to_experts(send_m), to_experts(send_c), gate_parts, up_parts, down_parts))
    grad_back = unfold_parts(grad_e)
    out_back = unfold_parts(out_e)
    spread_four = spread_b.reshape(N_EXPERT, TOK_DEV, EXPERTS, CAP)
    row_sum = jnp.einsum('ntec,ejncd->ntd', spread_four, grad_back, precision=lax.Precision.HIGHEST).reshape(TOKENS, D)
    place_five = place_b.reshape(N_EXPERT, TOK_DEV, TOP, EXPERTS, CAP)
    out_route = jnp.einsum('ntkec,ejncd->ntkd', place_five, out_back, precision=lax.Precision.HIGHEST).reshape(TOKENS, TOP, D)
    dgate = lax.optimization_barrier(jnp.sum(out_route * cotan.astype(jnp.float32)[:, None, :], axis=-1))
    bwd_result = token_grad(saved, cotan, norm_gain, router_w, chosen_b, total_b, share_b, pick_b, dgate, row_sum)
    return (fwd_result, bwd_result)

def reference(fwd_tokens, saved_tokens, cotangent, fwd_routes, bwd_routes, norm_gain, router, w_gate, w_up, w_down):
    forward_in = fwd_tokens
    cotan_in = cotangent
    for tick_index in range(TICKS):
        fwd_result, bwd_result = lax.map(section_step, (forward_in, saved_tokens[tick_index], cotan_in, fwd_routes[tick_index], bwd_routes[tick_index], norm_gain, router, w_gate, w_up, w_down))
        if tick_index + 1 < TICKS:
            forward_in = jnp.roll(fwd_result, 1, axis=0)
            cotan_in = jnp.roll(bwd_result, -1, axis=0)
    return (fwd_result, bwd_result)
```

```python
import jax
import jax.numpy as jnp
from jax import lax
from jax.sharding import PartitionSpec as P

BF16 = jnp.bfloat16
F32 = jnp.float32


def shift(block, axis, distance):
    size = lax.axis_size(axis)
    return lax.ppermute(block, axis, [((i - distance) % size, i) for i in range(size)])


def norm_rows(values, norm_gain):
    wide = values.astype(F32)
    scale = lax.rsqrt(jnp.mean(wide * wide, axis=-1, keepdims=True) + 1e-06)
    return wide * scale * norm_gain


def norm_pull(values, norm_gain, grad):
    wide = values.astype(F32)
    scale = lax.rsqrt(jnp.mean(wide * wide, axis=-1, keepdims=True) + 1e-06)
    scaled = grad * norm_gain
    inner = jnp.mean(scaled * wide, axis=-1, keepdims=True)
    return scale * (scaled - wide * (scale * scale) * inner)


def gate_values(normed, router_w, pick):
    logits = jnp.dot(normed, router_w, preferred_element_type=F32)
    sig_all = jax.nn.sigmoid(logits)
    chosen = jnp.sum(pick * sig_all[:, None, :], axis=-1)
    total = jnp.sum(chosen, axis=-1, keepdims=True)
    return chosen, total, chosen / total


def slot_places(routes, experts, cap):
    flat = routes.reshape(-1)
    hit = (flat[:, None] == jnp.arange(experts, dtype=jnp.int32)).astype(F32)
    count = flat.shape[0]
    earlier = (jnp.arange(count)[:, None] > jnp.arange(count)[None, :]).astype(F32)
    before = jnp.dot(earlier, hit, preferred_element_type=F32)
    slot = jnp.sum(before * hit, axis=1).astype(jnp.int32)
    place = hit[:, :, None] * (slot[:, None, None] == jnp.arange(cap, dtype=jnp.int32)).astype(F32)
    return place.reshape(routes.shape + (experts, cap))


def slab_sizes(width):
    return width // 2, width // 7


def pieces(rows, step):
    return jnp.concatenate([rows[:, i:i + step] for i in range(0, rows.shape[1], step)], axis=0)


def unpieces(stacked, count):
    tokens = stacked.shape[0] // count
    return jnp.concatenate([stacked[i * tokens:(i + 1) * tokens] for i in range(count)], axis=1)


def pack_rows(rows, spread, copies, scalars=None):
    tokens, width = rows.shape
    experts = spread.shape[1]
    half, piece = slab_sizes(width)
    eye2 = jnp.eye(2, dtype=F32)
    eye87 = jnp.eye(8, 7, dtype=F32)
    main = jnp.einsum("tes,hg->ehsgt", spread[:, :, :4], eye2).reshape(experts, 1, 8, 2 * tokens)
    tail = jnp.einsum("te,cd->ecdt", spread[:, :, 4], eye87).reshape(experts, 1, 8, 7 * tokens)
    main = jnp.broadcast_to(main, (experts, copies, 8, 2 * tokens)).reshape(-1, 2 * tokens)
    tail = jnp.broadcast_to(tail, (experts, copies, 8, 7 * tokens)).reshape(-1, 7 * tokens)
    out_main = jnp.dot(main.astype(BF16), pieces(rows, half), preferred_element_type=F32).astype(BF16)
    out_tail = jnp.dot(tail.astype(BF16), pieces(rows, piece), preferred_element_type=F32)
    if scalars is not None:
        extra = jnp.zeros((experts, 1, 8, piece), F32).at[:, 0, 7, :scalars.shape[1]].set(scalars)
        extra = jnp.broadcast_to(extra, (experts, copies, 8, piece)).reshape(-1, piece)
        out_tail = out_tail + extra
    slab = jnp.concatenate([out_main, out_tail.astype(BF16)], axis=1)
    return slab.reshape(experts * copies, 8, half + piece)


def combine_rows(slabs, weights):
    tokens, experts, cap = weights.shape
    copies = slabs.shape[0] // experts
    half = slabs.shape[2] * 7 // 9
    eye2 = jnp.eye(2, dtype=F32)
    eye78 = jnp.eye(7, 8, dtype=F32)
    flat = slabs.reshape(-1, slabs.shape[2])
    main = jnp.einsum("tes,gh->gtehs", weights[:, :, :4], eye2).reshape(2 * tokens, experts, 1, 8)
    tail = jnp.einsum("te,dc->dtec", weights[:, :, 4], eye78).reshape(7 * tokens, experts, 1, 8)
    main = jnp.broadcast_to(main, (2 * tokens, experts, copies, 8)).reshape(2 * tokens, -1)
    tail = jnp.broadcast_to(tail, (7 * tokens, experts, copies, 8)).reshape(7 * tokens, -1)
    sum_main = jnp.dot(main.astype(BF16), flat[:, :half], preferred_element_type=F32)
    sum_tail = jnp.dot(tail.astype(BF16), flat[:, half:], preferred_element_type=F32)
    return unpieces(sum_main, 2) + unpieces(sum_tail, 7)


def open_slabs(slabs):
    sources, _, full = slabs.shape
    half = full * 7 // 9
    first = jnp.concatenate([slabs[:, 0:4, :half], slabs[:, 4:8, :half]], axis=2)
    last = slabs[:, 0:7, half:].reshape(sources, -1)
    return jnp.concatenate([first.reshape(sources * 4, -1), last], axis=0)


def close_slabs(rows, sources, scalars=None):
    width = rows.shape[1]
    half, piece = slab_sizes(width)
    first = rows[:sources * 4].reshape(sources, 4, width)
    main = jnp.concatenate([first[:, :, :half], first[:, :, half:]], axis=1)
    last = rows[sources * 4:].reshape(sources, 7, piece)
    extra = jnp.zeros((sources, 1, piece), BF16)
    if scalars is not None:
        extra = extra.at[:, 0, :scalars.shape[1]].set(scalars.astype(BF16))
    tail = jnp.concatenate([last, extra], axis=1)
    return jnp.concatenate([main, tail], axis=2)


def slot_scalars(slabs, count, first=0):
    half = slabs.shape[2] * 7 // 9
    return slabs[:, 7, half + first:half + first + count].astype(F32)


def in_row_order(per_slot):
    sources = per_slot.shape[0]
    return jnp.concatenate([per_slot[:, :4].reshape(sources * 4), per_slot[:, 4]])


def in_slot_order(per_row, sources):
    return jnp.concatenate([per_row[:sources * 4].reshape(sources, 4), per_row[sources * 4:, None]], axis=1)


def expert_forward(slabs, gate_w, up_w, down_w):
    rows = open_slabs(slabs)
    gate_pre = jnp.dot(rows, gate_w, preferred_element_type=F32)
    up_pre = jnp.dot(rows, up_w, preferred_element_type=F32)
    hidden = (jax.nn.silu(gate_pre) * up_pre).astype(BF16)
    out = jnp.dot(hidden, down_w, preferred_element_type=F32).astype(BF16)
    return close_slabs(out, slabs.shape[0])


def expert_backward(saved_slabs, cot_slabs, gate_w, up_w, down_w):
    sources = saved_slabs.shape[0]
    rows = open_slabs(saved_slabs)
    cot = open_slabs(cot_slabs)
    gb = in_row_order(slot_scalars(cot_slabs, 5))
    gate_pre = jnp.dot(rows, gate_w, preferred_element_type=F32)
    up_pre = jnp.dot(rows, up_w, preferred_element_type=F32)
    gate_sig = jax.nn.sigmoid(gate_pre)
    gate_act = gate_pre * gate_sig
    hidden = (gate_act * up_pre).astype(BF16).astype(F32)
    cot_hidden = jnp.einsum("rd,fd->rf", cot, down_w, preferred_element_type=F32)
    dgate = jnp.sum(hidden * cot_hidden, axis=1)
    hidden_grad = cot_hidden * gb[:, None]
    gate_grad = (hidden_grad * up_pre * gate_sig * (1.0 + gate_pre * (1.0 - gate_sig))).astype(BF16)
    up_grad = (hidden_grad * gate_act).astype(BF16)
    row_grad = jnp.einsum("rf,df->rd", gate_grad, gate_w, preferred_element_type=F32)
    row_grad = row_grad + jnp.einsum("rf,df->rd", up_grad, up_w, preferred_element_type=F32)
    dgate = in_slot_order(dgate, sources)
    high = lax.reduce_precision(dgate, 8, 7)
    low = dgate - high
    return close_slabs(row_grad.astype(BF16), sources, jnp.concatenate([high, low], axis=1))


def local(
    fwd_tokens,
    saved_tokens,
    cotangent,
    fwd_routes,
    bwd_routes,
    norm_gain,
    router,
    w_gate,
    w_up,
    w_down,
):
    gain = norm_gain[0]
    router_w = router[0]
    ticks = saved_tokens.shape[0]
    tokens = fwd_tokens.shape[1]
    top = fwd_routes.shape[-1]
    experts = router_w.shape[1]
    cap = 5 * tokens * top // (4 * experts)
    ranks = lax.axis_size("expert")
    depth = ranks // 2
    copies = depth // experts
    columns = [[x + 2 * z for z in range(depth)] for x in range(2)]
    partner = [(i, i ^ 1) for i in range(ranks)]

    def exchange(slabs):
        return lax.all_to_all(
            slabs, "expert", split_axis=0, concat_axis=0, axis_index_groups=columns, tiled=True
        )

    gate_w = jnp.concatenate([w_gate[0], lax.ppermute(w_gate[0], "expert", partner)], axis=1)
    up_w = jnp.concatenate([w_up[0], lax.ppermute(w_up[0], "expert", partner)], axis=1)
    down_w = jnp.concatenate([w_down[0], lax.ppermute(w_down[0], "expert", partner)], axis=0)

    forward_in = fwd_tokens[0]
    cotan_in = cotangent[0]
    expert_ids = jnp.arange(experts, dtype=jnp.int32)
    saved_parts = []
    for t in range(ticks):
        saved = saved_tokens[t, 0]
        saved_norm = norm_rows(saved, gain).astype(BF16)
        pick = (bwd_routes[t, 0][..., None] == expert_ids).astype(F32)
        place = slot_places(bwd_routes[t, 0], experts, cap)
        chosen, total, share = gate_values(saved_norm, router_w, pick)
        gb = share.astype(BF16).astype(F32)
        spread = jnp.sum(place, axis=1)
        slot_gb = jnp.sum(place * gb[:, :, None, None], axis=(0, 1))
        saved_parts.append((saved, saved_norm, pick, place, chosen, total, share, spread, slot_gb))

    for t in range(ticks):
        saved, saved_norm, pick, place, chosen, total, share, spread, slot_gb = saved_parts[t]
        normed = norm_rows(forward_in, gain).astype(BF16)
        place_f = slot_places(fwd_routes[t, 0], experts, cap)
        pick_f = (fwd_routes[t, 0][..., None] == expert_ids).astype(F32)
        rows_f = exchange(pack_rows(normed, jnp.sum(place_f, axis=1), copies))
        rows_m = exchange(pack_rows(saved_norm, spread, copies))
        rows_c = exchange(pack_rows(cotan_in, spread, copies, slot_gb))
        _, _, share_f = gate_values(normed, router_w, pick_f)
        gb_f = share_f.astype(BF16).astype(F32)
        weights_f = jnp.sum(place_f * gb_f[:, :, None, None], axis=1)
        back_f = exchange(expert_forward(rows_f, gate_w, up_w, down_w))
        back_b = exchange(expert_backward(rows_m, rows_c, gate_w, up_w, down_w))

        fwd_result = (forward_in.astype(F32) + combine_rows(back_f, weights_f)).astype(BF16)

        row_sum = combine_rows(back_b, spread)
        slot_dgate = slot_scalars(back_b, cap) + slot_scalars(back_b, cap, cap)
        slot_dgate = jnp.sum(slot_dgate.reshape(experts, copies, cap), axis=1)
        dgate = jnp.sum(place * slot_dgate, axis=(2, 3))
        dchosen = (dgate - jnp.sum(share * dgate, axis=-1, keepdims=True)) / total
        logit_grad = dchosen * chosen * (1.0 - chosen)
        logit_full = jnp.sum(logit_grad[:, :, None] * pick, axis=1)
        router_back = jnp.dot(logit_full, router_w.astype(F32).T, precision=lax.Precision.HIGHEST)
        pulled = norm_pull(saved, gain, row_sum + router_back)
        bwd_result = (cotan_in.astype(F32) + pulled).astype(BF16)
        if t + 1 < ticks:
            forward_in = shift(fwd_result, "pipe", 1)
            cotan_in = shift(bwd_result, "pipe", -1)
    return (fwd_result[None], bwd_result[None])


def solution(mesh):
    return jax.shard_map(
        local,
        mesh=mesh,
        in_specs=(
            P("pipe", "expert", None),
            P(None, "pipe", "expert", None),
            P("pipe", "expert", None),
            P(None, "pipe", "expert", None),
            P(None, "pipe", "expert", None),
            P("pipe", None),
            P("pipe", None, None),
            P("pipe", None, "expert"),
            P("pipe", None, "expert"),
            P("pipe", "expert", None),
        ),
        out_specs=(P("pipe", "expert", None), P("pipe", "expert", None)),
        check_vma=False,
    )
```

```python
import jax
import jax.numpy as jnp
from jax import lax
from jax.sharding import PartitionSpec as P

BF16 = jnp.bfloat16
F32 = jnp.float32


def shift(block, axis, distance):
    size = lax.axis_size(axis)
    return lax.ppermute(block, axis, [((i - distance) % size, i) for i in range(size)])


def norm_rows(values, norm_gain):
    wide = values.astype(F32)
    scale = lax.rsqrt(jnp.mean(wide * wide, axis=-1, keepdims=True) + 1e-06)
    return wide * scale * norm_gain


def norm_pull(values, norm_gain, grad):
    wide = values.astype(F32)
    scale = lax.rsqrt(jnp.mean(wide * wide, axis=-1, keepdims=True) + 1e-06)
    scaled = grad * norm_gain
    inner = jnp.mean(scaled * wide, axis=-1, keepdims=True)
    return scale * (scaled - wide * (scale * scale) * inner)


def gate_values(normed, router_w, pick):
    logits = jnp.dot(normed, router_w, preferred_element_type=F32)
    sig_all = jax.nn.sigmoid(logits)
    chosen = jnp.sum(pick * sig_all[:, None, :], axis=-1)
    total = jnp.sum(chosen, axis=-1, keepdims=True)
    return chosen, total, chosen / total


def slot_places(routes, experts, cap):
    flat = routes.reshape(-1)
    hit = (flat[:, None] == jnp.arange(experts, dtype=jnp.int32)).astype(F32)
    count = flat.shape[0]
    earlier = (jnp.arange(count)[:, None] > jnp.arange(count)[None, :]).astype(F32)
    before = jnp.dot(earlier, hit, preferred_element_type=F32)
    slot = jnp.sum(before * hit, axis=1).astype(jnp.int32)
    place = hit[:, :, None] * (slot[:, None, None] == jnp.arange(cap, dtype=jnp.int32)).astype(F32)
    return place.reshape(routes.shape + (experts, cap))


def slab_sizes(width):
    return width // 2, width // 7


def pieces(rows, step):
    return jnp.concatenate([rows[:, i:i + step] for i in range(0, rows.shape[1], step)], axis=0)


def unpieces(stacked, count):
    tokens = stacked.shape[0] // count
    return jnp.concatenate([stacked[i * tokens:(i + 1) * tokens] for i in range(count)], axis=1)


def pack_rows(rows, spread, copies, scalars=None):
    tokens, width = rows.shape
    experts = spread.shape[1]
    half, piece = slab_sizes(width)
    eye2 = jnp.eye(2, dtype=F32)
    eye87 = jnp.eye(8, 7, dtype=F32)
    main = jnp.einsum("tes,hg->ehsgt", spread[:, :, :4], eye2).reshape(experts, 1, 8, 2 * tokens)
    tail = jnp.einsum("te,cd->ecdt", spread[:, :, 4], eye87).reshape(experts, 1, 8, 7 * tokens)
    main = jnp.broadcast_to(main, (experts, copies, 8, 2 * tokens)).reshape(-1, 2 * tokens)
    tail = jnp.broadcast_to(tail, (experts, copies, 8, 7 * tokens)).reshape(-1, 7 * tokens)
    out_main = jnp.dot(main.astype(BF16), pieces(rows, half), preferred_element_type=F32).astype(BF16)
    out_tail = jnp.dot(tail.astype(BF16), pieces(rows, piece), preferred_element_type=F32)
    if scalars is not None:
        extra = jnp.zeros((experts, 1, 8, piece), F32).at[:, 0, 7, :scalars.shape[1]].set(scalars)
        extra = jnp.broadcast_to(extra, (experts, copies, 8, piece)).reshape(-1, piece)
        out_tail = out_tail + extra
    slab = jnp.concatenate([out_main, out_tail.astype(BF16)], axis=1)
    return slab.reshape(experts * copies, 8, half + piece)


def combine_rows(slabs, weights):
    tokens, experts, cap = weights.shape
    copies = slabs.shape[0] // experts
    half = slabs.shape[2] * 7 // 9
    eye2 = jnp.eye(2, dtype=F32)
    eye78 = jnp.eye(7, 8, dtype=F32)
    flat = slabs.reshape(-1, slabs.shape[2])
    main = jnp.einsum("tes,gh->gtehs", weights[:, :, :4], eye2).reshape(2 * tokens, experts, 1, 8)
    tail = jnp.einsum("te,dc->dtec", weights[:, :, 4], eye78).reshape(7 * tokens, experts, 1, 8)
    main = jnp.broadcast_to(main, (2 * tokens, experts, copies, 8)).reshape(2 * tokens, -1)
    tail = jnp.broadcast_to(tail, (7 * tokens, experts, copies, 8)).reshape(7 * tokens, -1)
    sum_main = jnp.dot(main.astype(BF16), flat[:, :half], preferred_element_type=F32)
    sum_tail = jnp.dot(tail.astype(BF16), flat[:, half:], preferred_element_type=F32)
    return unpieces(sum_main, 2) + unpieces(sum_tail, 7)


def open_slabs(slabs):
    sources, _, full = slabs.shape
    half = full * 7 // 9
    first = jnp.concatenate([slabs[:, 0:4, :half], slabs[:, 4:8, :half]], axis=2)
    last = slabs[:, 0:7, half:].reshape(sources, -1)
    return jnp.concatenate([first.reshape(sources * 4, -1), last], axis=0)


def close_slabs(rows, sources, scalars=None):
    width = rows.shape[1]
    half, piece = slab_sizes(width)
    first = rows[:sources * 4].reshape(sources, 4, width)
    main = jnp.concatenate([first[:, :, :half], first[:, :, half:]], axis=1)
    last = rows[sources * 4:].reshape(sources, 7, piece)
    extra = jnp.zeros((sources, 1, piece), BF16)
    if scalars is not None:
        extra = extra.at[:, 0, :scalars.shape[1]].set(scalars.astype(BF16))
    tail = jnp.concatenate([last, extra], axis=1)
    return jnp.concatenate([main, tail], axis=2)


def slot_scalars(slabs, count, first=0):
    half = slabs.shape[2] * 7 // 9
    return slabs[:, 7, half + first:half + first + count].astype(F32)


def in_row_order(per_slot):
    sources = per_slot.shape[0]
    return jnp.concatenate([per_slot[:, :4].reshape(sources * 4), per_slot[:, 4]])


def in_slot_order(per_row, sources):
    return jnp.concatenate([per_row[:sources * 4].reshape(sources, 4), per_row[sources * 4:, None]], axis=1)


def expert_forward(slabs, gate_w, up_w, down_w):
    rows = open_slabs(slabs)
    gate_pre = jnp.dot(rows, gate_w, preferred_element_type=F32)
    up_pre = jnp.dot(rows, up_w, preferred_element_type=F32)
    hidden = (jax.nn.silu(gate_pre) * up_pre).astype(BF16)
    out = jnp.dot(hidden, down_w, preferred_element_type=F32).astype(BF16)
    return close_slabs(out, slabs.shape[0])


def expert_backward(saved_slabs, cot_slabs, part, parts, gate_w, up_w, down_w):
    sources = saved_slabs.shape[0]
    rows = open_slabs(saved_slabs)
    cot = open_slabs(cot_slabs)
    gb = in_row_order(slot_scalars(saved_slabs, 5))
    gate_pre = jnp.dot(rows, gate_w, preferred_element_type=F32)
    up_pre = jnp.dot(rows, up_w, preferred_element_type=F32)
    gate_sig = jax.nn.sigmoid(gate_pre)
    gate_act = gate_pre * gate_sig
    hidden = (gate_act * up_pre).astype(BF16).astype(F32)
    cot_hidden = jnp.einsum("rd,fd->rf", cot, down_w, preferred_element_type=F32)
    dgate = jnp.sum(hidden * cot_hidden, axis=1)
    hidden_grad = cot_hidden * gb[:, None]
    gate_grad = (hidden_grad * up_pre * gate_sig * (1.0 + gate_pre * (1.0 - gate_sig))).astype(BF16)
    up_grad = (hidden_grad * gate_act).astype(BF16)
    row_grad = jnp.einsum("rf,df->rd", gate_grad, gate_w, preferred_element_type=F32)
    row_grad = row_grad + jnp.einsum("rf,df->rd", up_grad, up_w, preferred_element_type=F32)
    dgate = in_slot_order(dgate, sources)
    high = lax.reduce_precision(dgate, 8, 7)
    both = jnp.concatenate([high, dgate - high], axis=1)
    mine = (jnp.arange(parts) == part).astype(F32)
    scalars = (mine[None, :, None] * both[:, None, :]).reshape(sources, -1)
    return close_slabs(row_grad.astype(BF16), sources, scalars)


def local(
    fwd_tokens,
    saved_tokens,
    cotangent,
    fwd_routes,
    bwd_routes,
    norm_gain,
    router,
    w_gate,
    w_up,
    w_down,
):
    gain = norm_gain[0]
    router_w = router[0]
    ticks = saved_tokens.shape[0]
    tokens = fwd_tokens.shape[1]
    top = fwd_routes.shape[-1]
    experts = router_w.shape[1]
    cap = 5 * tokens * top // (4 * experts)
    ranks = lax.axis_size("expert")
    depth = ranks // 2
    copies = depth // experts
    partner = [(i, i ^ 1) for i in range(ranks)]
    far = [[x + 2 * (p + copies * e) for e in range(experts)] for p in range(copies) for x in range(2)]
    near = [[x + 2 * (p + copies * e) for p in range(copies)] for e in range(experts) for x in range(2)]
    part = lax.axis_index("expert") // 2 % copies

    def swap(slabs, groups):
        return lax.all_to_all(
            slabs, "expert", split_axis=0, concat_axis=0, axis_index_groups=groups, tiled=True
        )

    def dispatch(*slabs):
        held = swap(jnp.concatenate(slabs, axis=1), far)
        spread = swap(jnp.broadcast_to(held[None], (copies,) + held.shape), near)
        spread = spread.reshape((depth,) + held.shape[1:])
        return [spread[:, 8 * i:8 * i + 8] for i in range(len(slabs))]

    def gather_back(*slabs):
        parts = jnp.concatenate(slabs, axis=1)
        parts = swap(parts.reshape((copies, experts) + parts.shape[1:]), near)
        held = swap(jnp.sum(parts.astype(F32), axis=0).astype(BF16), far)
        return [held[:, 8 * i:8 * i + 8] for i in range(len(slabs))]

    def after(value, *earlier):
        return lax.optimization_barrier((value,) + earlier)[0]

    gate_r = lax.ppermute(w_gate[0], "expert", partner)
    up_r = lax.ppermute(w_up[0], "expert", partner)
    down_r = lax.ppermute(w_down[0], "expert", partner)

    expert_ids = jnp.arange(experts, dtype=jnp.int32)
    fwd_places = [slot_places(fwd_routes[t, 0], experts, cap) for t in range(ticks)]
    bwd_places = [slot_places(bwd_routes[t, 0], experts, cap) for t in range(ticks)]
    fwd_spreads = [jnp.sum(place, axis=1) for place in fwd_places]
    bwd_spreads = [jnp.sum(place, axis=1) for place in bwd_places]

    def pack_saved(t):
        saved = saved_tokens[t, 0]
        saved_norm = norm_rows(saved, gain).astype(BF16)
        pick = (bwd_routes[t, 0][..., None] == expert_ids).astype(F32)
        chosen, total, share = gate_values(saved_norm, router_w, pick)
        gb = share.astype(BF16).astype(F32)
        slot_gb = jnp.sum(bwd_places[t] * gb[:, :, None, None], axis=(0, 1))
        slabs = pack_rows(saved_norm, bwd_spreads[t], 1, slot_gb)
        return slabs, (saved, pick, chosen, total, share)

    def finish_forward(t, tokens_in, normed, back):
        pick = (fwd_routes[t, 0][..., None] == expert_ids).astype(F32)
        _, _, share = gate_values(normed, router_w, pick)
        gb = share.astype(BF16).astype(F32)
        weights = jnp.sum(fwd_places[t] * gb[:, :, None, None], axis=1)
        return (tokens_in.astype(F32) + combine_rows(back, weights)).astype(BF16)

    def finish_backward(t, cot, parts, back):
        saved, pick, chosen, total, share = parts
        row_sum = combine_rows(back, bwd_spreads[t])
        slot_dgate = slot_scalars(back, copies * 2 * cap).reshape(experts, copies * 2, cap).sum(axis=1)
        dgate = jnp.sum(bwd_places[t] * slot_dgate, axis=(2, 3))
        dchosen = (dgate - jnp.sum(share * dgate, axis=-1, keepdims=True)) / total
        logit_grad = dchosen * chosen * (1.0 - chosen)
        logit_full = jnp.sum(logit_grad[:, :, None] * pick, axis=1)
        router_back = jnp.dot(logit_full, router_w.astype(F32).T, precision=lax.Precision.HIGHEST)
        return (cot.astype(F32) + norm_pull(saved, gain, row_sum + router_back)).astype(BF16)

    forward_in = fwd_tokens[0]
    cotan_in = cotangent[0]
    normed = norm_rows(forward_in, gain).astype(BF16)
    packed = [pack_saved(t) for t in range(ticks)]
    rows_f, rows_c, *rows_m = dispatch(
        pack_rows(normed, fwd_spreads[0], 1),
        pack_rows(cotan_in, bwd_spreads[0], 1),
        *[slabs for slabs, _ in packed],
    )
    weights = (
        jnp.concatenate([w_gate[0], gate_r], axis=1),
        jnp.concatenate([w_up[0], up_r], axis=1),
        jnp.concatenate([w_down[0], down_r], axis=0),
    )
    for t in range(ticks):
        back_f, back_b = gather_back(
            expert_forward(rows_f, *weights),
            expert_backward(rows_m[t], rows_c, part, copies, *weights),
        )
        fwd_result = finish_forward(t, forward_in, normed, back_f)
        bwd_result = finish_backward(t, cotan_in, packed[t][1], back_b)
        if t + 1 < ticks:
            forward_in = shift(fwd_result, "pipe", 1)
            cotan_in = shift(bwd_result, "pipe", -1)
            normed = norm_rows(forward_in, gain).astype(BF16)
            rows_f, rows_c = dispatch(
                pack_rows(normed, fwd_spreads[t + 1], 1),
                pack_rows(cotan_in, bwd_spreads[t + 1], 1),
            )
    return (fwd_result[None], bwd_result[None])


def solution(mesh):
    return jax.shard_map(
        local,
        mesh=mesh,
        in_specs=(
            P("pipe", "expert", None),
            P(None, "pipe", "expert", None),
            P("pipe", "expert", None),
            P(None, "pipe", "expert", None),
            P(None, "pipe", "expert", None),
            P("pipe", None),
            P("pipe", None, None),
            P("pipe", None, "expert"),
            P("pipe", None, "expert"),
            P("pipe", "expert", None),
        ),
        out_specs=(P("pipe", "expert", None), P("pipe", "expert", None)),
        check_vma=False,
    )
```

```python
import functools

import jax
import jax.numpy as jnp
from jax import lax
from jax.experimental import pallas as pl
from jax.experimental.pallas import tpu as pltpu
from jax.sharding import PartitionSpec as P

BF16 = jnp.bfloat16
F32 = jnp.float32


def shift(block, axis, distance):
    size = lax.axis_size(axis)
    return lax.ppermute(block, axis, [((i - distance) % size, i) for i in range(size)])


def norm_rows(values, norm_gain):
    wide = values.astype(F32)
    scale = lax.rsqrt(jnp.mean(wide * wide, axis=-1, keepdims=True) + 1e-06)
    return wide * scale * norm_gain


def norm_pull(values, norm_gain, grad):
    wide = values.astype(F32)
    scale = lax.rsqrt(jnp.mean(wide * wide, axis=-1, keepdims=True) + 1e-06)
    scaled = grad * norm_gain
    inner = jnp.mean(scaled * wide, axis=-1, keepdims=True)
    return scale * (scaled - wide * (scale * scale) * inner)


def gate_values(normed, router_w, pick):
    logits = jnp.dot(normed, router_w, preferred_element_type=F32)
    sig_all = jax.nn.sigmoid(logits)
    chosen = jnp.sum(pick * sig_all[:, None, :], axis=-1)
    total = jnp.sum(chosen, axis=-1, keepdims=True)
    return chosen, total, chosen / total


def slot_places(routes, experts, cap):
    flat = routes.reshape(-1)
    hit = (flat[:, None] == jnp.arange(experts, dtype=jnp.int32)).astype(F32)
    count = flat.shape[0]
    earlier = (jnp.arange(count)[:, None] > jnp.arange(count)[None, :]).astype(F32)
    before = jnp.dot(earlier, hit, preferred_element_type=F32)
    slot = jnp.sum(before * hit, axis=1).astype(jnp.int32)
    place = hit[:, :, None] * (slot[:, None, None] == jnp.arange(cap, dtype=jnp.int32)).astype(F32)
    return place.reshape(routes.shape + (experts, cap))


def slab_sizes(width):
    return width // 2, width // 7


def pieces(rows, step):
    return jnp.concatenate([rows[:, i:i + step] for i in range(0, rows.shape[1], step)], axis=0)


def unpieces(stacked, count):
    tokens = stacked.shape[0] // count
    return jnp.concatenate([stacked[i * tokens:(i + 1) * tokens] for i in range(count)], axis=1)


def pack_rows(rows, spread, copies, scalars=None):
    tokens, width = rows.shape
    experts = spread.shape[1]
    half, piece = slab_sizes(width)
    eye2 = jnp.eye(2, dtype=F32)
    eye87 = jnp.eye(8, 7, dtype=F32)
    main = jnp.einsum("tes,hg->ehsgt", spread[:, :, :4], eye2).reshape(experts, 1, 8, 2 * tokens)
    tail = jnp.einsum("te,cd->ecdt", spread[:, :, 4], eye87).reshape(experts, 1, 8, 7 * tokens)
    main = jnp.broadcast_to(main, (experts, copies, 8, 2 * tokens)).reshape(-1, 2 * tokens)
    tail = jnp.broadcast_to(tail, (experts, copies, 8, 7 * tokens)).reshape(-1, 7 * tokens)
    out_main = jnp.dot(main.astype(BF16), pieces(rows, half), preferred_element_type=F32).astype(BF16)
    out_tail = jnp.dot(tail.astype(BF16), pieces(rows, piece), preferred_element_type=F32)
    if scalars is not None:
        extra = jnp.zeros((experts, 1, 8, piece), F32).at[:, 0, 7, :scalars.shape[1]].set(scalars)
        extra = jnp.broadcast_to(extra, (experts, copies, 8, piece)).reshape(-1, piece)
        out_tail = out_tail + extra
    slab = jnp.concatenate([out_main, out_tail.astype(BF16)], axis=1)
    return slab.reshape(experts * copies, 8, half + piece)


def combine_rows(slabs, weights):
    tokens, experts, cap = weights.shape
    copies = slabs.shape[0] // experts
    half = slabs.shape[2] * 7 // 9
    eye2 = jnp.eye(2, dtype=F32)
    eye78 = jnp.eye(7, 8, dtype=F32)
    flat = slabs.reshape(-1, slabs.shape[2])
    main = jnp.einsum("tes,gh->gtehs", weights[:, :, :4], eye2).reshape(2 * tokens, experts, 1, 8)
    tail = jnp.einsum("te,dc->dtec", weights[:, :, 4], eye78).reshape(7 * tokens, experts, 1, 8)
    main = jnp.broadcast_to(main, (2 * tokens, experts, copies, 8)).reshape(2 * tokens, -1)
    tail = jnp.broadcast_to(tail, (7 * tokens, experts, copies, 8)).reshape(7 * tokens, -1)
    sum_main = jnp.dot(main.astype(BF16), flat[:, :half], preferred_element_type=F32)
    sum_tail = jnp.dot(tail.astype(BF16), flat[:, half:], preferred_element_type=F32)
    return unpieces(sum_main, 2) + unpieces(sum_tail, 7)


def slot_scalars(slabs, count):
    half = slabs.shape[2] * 7 // 9
    return slabs[:, 7, half:half + count].astype(F32)


SOURCES = 16


def iota(shape, dim):
    return lax.broadcasted_iota(jnp.int32, shape, dim)


def one_hot(wanted, held):
    return jnp.where(wanted == held, 1.0, 0.0).astype(BF16)


def main_place(r):
    return (((r >> 2) & (SOURCES - 1)) << 3) | ((r >> 6) << 2) | (r & 3)


def tail_place(r):
    return ((r & (SOURCES - 1)) << 3) | (r >> 4)


def row_source(r):
    return jnp.where(r < 4 * SOURCES, r >> 2, r - 4 * SOURCES)


def row_slot(r):
    return jnp.where(r < 4 * SOURCES, r & 3, 4)


def dot(left, right, left_dim=1, right_dim=0):
    return lax.dot_general(
        left, right, (((left_dim,), (right_dim,)), ((), ())), preferred_element_type=F32
    )


def unpack(slabs, rows_ref):
    half, piece = slab_sizes(rows_ref.shape[1])
    count = 4 * SOURCES
    pick = one_hot(main_place(iota((2 * count, 8 * SOURCES), 0)), iota((2 * count, 8 * SOURCES), 1))
    main = dot(pick, slabs[:, :half]).astype(BF16)
    rows_ref[:count, :half] = main[:count]
    rows_ref[:count, half:] = main[count:]
    pick = one_hot(tail_place(iota((7 * SOURCES, 8 * SOURCES), 0)), iota((7 * SOURCES, 8 * SOURCES), 1))
    tail = dot(pick, slabs[:, half:]).astype(BF16)
    for i in range(7):
        rows_ref[count:, i * piece:(i + 1) * piece] = tail[i * SOURCES:(i + 1) * SOURCES]


def pack(rows, keep_ref, send_ref, scalars=None):
    half, piece = slab_sizes(rows.shape[1])
    count = 4 * SOURCES
    stacked = jnp.concatenate([rows[:count, :half], rows[:count, half:]], axis=0)
    pick = one_hot(main_place(iota((8 * SOURCES, 2 * count), 1)), iota((8 * SOURCES, 2 * count), 0))
    main = dot(pick, stacked).astype(BF16)
    stacked = jnp.concatenate([rows[count:, i * piece:(i + 1) * piece] for i in range(7)], axis=0)
    pick = one_hot(tail_place(iota((8 * SOURCES, 7 * SOURCES), 1)), iota((8 * SOURCES, 7 * SOURCES), 0))
    tail = dot(pick, stacked)
    mid = keep_ref.shape[0]
    keep_ref[:, :half] = main[:mid]
    send_ref[:, :half] = main[mid:]
    lanes = 0
    if scalars is not None:
        lanes = scalars.shape[1]
        first = (tail[:, :lanes] + scalars).astype(BF16)
        keep_ref[:, half:half + lanes] = first[:mid]
        send_ref[:, half:half + lanes] = first[mid:]
    tail = tail[:, lanes:].astype(BF16)
    keep_ref[:, half + lanes:] = tail[:mid]
    send_ref[:, half + lanes:] = tail[mid:]


def forward_kernel(near_ref, other_ref, gate_ref, up_ref, down_ref, keep_ref, send_ref, rows_ref):
    unpack(jnp.concatenate([near_ref[...], other_ref[...]], axis=0), rows_ref)
    rows = rows_ref[...]
    gate_pre = dot(rows, gate_ref[...])
    up_pre = dot(rows, up_ref[...])
    hidden = (gate_pre * jax.nn.sigmoid(gate_pre) * up_pre).astype(BF16)
    pack(dot(hidden, down_ref[...]).astype(BF16), keep_ref, send_ref)


def backward_kernel(
    tick, tokens, ticks, part_ref, saved_ref, near_ref, other_ref, gate_ref, up_ref, down_ref,
    keep_ref, send_ref, rows_ref,
):
    part = part_ref[0]
    slabs = jnp.concatenate([near_ref[...], other_ref[...]], axis=0)
    count = 5 * SOURCES
    half = slab_sizes(rows_ref.shape[1])[0]
    lanes = 128
    pick = one_hot((row_source(iota((count, 8 * SOURCES), 0)) << 3) | 7, iota((count, 8 * SOURCES), 1))
    scalars = dot(pick, slabs[:, half:half + lanes])
    slot = row_slot(iota((count, lanes), 0))
    lane = iota((count, lanes), 1)
    gb = jnp.sum(jnp.where(lane == slot, scalars, 0.0), axis=1, keepdims=True)
    token = jnp.sum(jnp.where(lane == slot + 5, scalars, 0.0), axis=1, keepdims=True).astype(jnp.int32)
    source = row_source(iota((count, 1), 0))
    away = (((source >> 2) & 1) << 1) | (source >> 3)
    depth_place = (away ^ part) + ((source & 3) << 2)
    first = depth_place * (ticks * tokens) + tick * tokens
    wanted = jnp.where(token < 0, -1, first + token)
    pick = one_hot(wanted, iota((count, saved_ref.shape[0]), 1))
    rows = dot(pick, saved_ref[...]).astype(BF16)
    unpack(slabs, rows_ref)
    cot_hidden = dot(rows_ref[...], down_ref[...], 1, 1)
    gate_pre = dot(rows, gate_ref[...])
    up_pre = dot(rows, up_ref[...])
    gate_sig = jax.nn.sigmoid(gate_pre)
    gate_act = gate_pre * gate_sig
    hidden = (gate_act * up_pre).astype(BF16).astype(F32)
    dgate = jnp.sum(hidden * cot_hidden, axis=1, keepdims=True)
    hidden_grad = cot_hidden * gb
    gate_grad = (hidden_grad * up_pre * gate_sig * (1.0 + gate_pre * (1.0 - gate_sig))).astype(BF16)
    up_grad = (hidden_grad * gate_act).astype(BF16)
    grad = dot(gate_grad, gate_ref[...], 1, 1) + dot(up_grad, up_ref[...], 1, 1)
    high = dgate.astype(BF16).astype(F32)
    own = lane - part * 10
    both = jnp.where(own == slot, high, jnp.where(own == slot + 5, dgate - high, 0.0)).astype(BF16)
    place = one_hot((row_source(iota((8 * SOURCES, count), 1)) << 3) | 7, iota((8 * SOURCES, count), 0))
    pack(grad.astype(BF16), keep_ref, send_ref, dot(place, both))


def run_kernel(kernel, slabs, operands, width, products, scalars=()):
    near, other = [slab.reshape(-1, slab.shape[2]) for slab in slabs]
    vmem = pl.BlockSpec(memory_space=pltpu.VMEM)
    inputs = [*operands[:-3], near, other, *operands[-3:]]
    moved = sum(value.size * value.dtype.itemsize for value in inputs) + 2 * near.size * 2
    units = operands[-1].shape[0]
    out = pl.pallas_call(
        kernel,
        out_shape=[jax.ShapeDtypeStruct(near.shape, BF16)] * 2,
        in_specs=[pl.BlockSpec(memory_space=pltpu.SMEM)] * len(scalars) + [vmem] * len(inputs),
        out_specs=[vmem] * 2,
        scratch_shapes=[pltpu.VMEM((5 * SOURCES, width), BF16)],
        compiler_params=pltpu.CompilerParams(vmem_limit_bytes=16 << 20),
        cost_estimate=pl.CostEstimate(
            flops=2 * products * 5 * SOURCES * width * units, bytes_accessed=moved, transcendentals=0
        ),
    )(*scalars, *inputs)
    return [value.reshape(slabs[0].shape) for value in out]


def local(
    fwd_tokens,
    saved_tokens,
    cotangent,
    fwd_routes,
    bwd_routes,
    norm_gain,
    router,
    w_gate,
    w_up,
    w_down,
):
    gain = norm_gain[0]
    router_w = router[0]
    ticks = saved_tokens.shape[0]
    tokens, width = fwd_tokens.shape[1:]
    top = fwd_routes.shape[-1]
    experts = router_w.shape[1]
    cap = 5 * tokens * top // (4 * experts)
    ranks = lax.axis_size("expert")
    depth = ranks // 2
    copies = depth // experts
    partner = [(i, i ^ 1) for i in range(ranks)]
    far = [[x + 2 * (p + copies * e) for e in range(experts)] for p in range(copies) for x in range(2)]
    column = [[x + 2 * z for z in range(depth)] for x in range(2)]
    part = lax.axis_index("expert") // 2 % copies

    def swap(slabs, groups):
        return lax.all_to_all(
            slabs, "expert", split_axis=0, concat_axis=0, axis_index_groups=groups, tiled=True
        )

    def after(value, *earlier):
        return lax.optimization_barrier((value,) + earlier)[0]

    def across(value, bit):
        return lax.ppermute(value, "expert", [(i, i ^ (2 * bit)) for i in range(ranks)])

    def spread_near(held, then=()):
        near = after(jnp.concatenate([held, across(held, 2)], axis=0), *then)
        return near, across(near, 1)

    def add(left, right):
        return (left.astype(F32) + right.astype(F32)).astype(BF16)

    def gather_near(keep, send):
        parts = add(keep, across(send, 1))
        count = parts.shape[0] // 2
        return add(parts[:count], across(parts[count:], 2))

    def dispatch(*slabs, first=(), then=((), ())):
        held = swap(after(jnp.concatenate(slabs, axis=1), *first), far)
        return [spread_near(held[:, 8 * i:8 * i + 8], then[i]) for i in range(len(slabs))]

    def gather_back(*slabs):
        held = swap(jnp.concatenate([gather_near(*slab) for slab in slabs], axis=1), far)
        return [held[:, 8 * i:8 * i + 8] for i in range(len(slabs))]

    half = w_gate.shape[1] // 2
    gate_r0 = lax.ppermute(w_gate[0, :half], "expert", partner)
    gate_r1 = lax.ppermute(after(w_gate[0, half:], gate_r0), "expert", partner)
    up_r = lax.ppermute(after(w_up[0], gate_r0), "expert", partner)
    down_r = lax.ppermute(after(w_down[0], gate_r1, up_r), "expert", partner)
    gate_r = jnp.concatenate([gate_r0, gate_r1], axis=0)

    expert_ids = jnp.arange(experts, dtype=jnp.int32)
    fwd_places = [slot_places(fwd_routes[t, 0], experts, cap) for t in range(ticks)]
    bwd_places = [slot_places(bwd_routes[t, 0], experts, cap) for t in range(ticks)]
    fwd_spreads = [jnp.sum(place, axis=1) for place in fwd_places]
    bwd_spreads = [jnp.sum(place, axis=1) for place in bwd_places]

    def saved_parts(t):
        saved = saved_tokens[t, 0]
        saved_norm = norm_rows(saved, gain).astype(BF16)
        pick = (bwd_routes[t, 0][..., None] == expert_ids).astype(F32)
        chosen, total, share = gate_values(saved_norm, router_w, pick)
        gb = share.astype(BF16).astype(F32)
        slot_gb = jnp.sum(bwd_places[t] * gb[:, :, None, None], axis=(0, 1))
        ids = jnp.arange(1, tokens + 1, dtype=F32)
        slot_token = jnp.sum(bwd_spreads[t] * ids[:, None, None], axis=0) - 1.0
        scalars = jnp.concatenate([slot_gb, slot_token], axis=1)
        return saved_norm, scalars, (saved, pick, chosen, total, share)

    def finish_forward(t, tokens_in, normed, back):
        pick = (fwd_routes[t, 0][..., None] == expert_ids).astype(F32)
        _, _, share = gate_values(normed, router_w, pick)
        gb = share.astype(BF16).astype(F32)
        weights = jnp.sum(fwd_places[t] * gb[:, :, None, None], axis=1)
        return (tokens_in.astype(F32) + combine_rows(back, weights)).astype(BF16)

    def finish_backward(t, cot, parts, back):
        saved, pick, chosen, total, share = parts
        row_sum = combine_rows(back, bwd_spreads[t])
        slot_dgate = slot_scalars(back, copies * 2 * cap).reshape(experts, copies * 2, cap).sum(axis=1)
        dgate = jnp.sum(bwd_places[t] * slot_dgate, axis=(2, 3))
        dchosen = (dgate - jnp.sum(share * dgate, axis=-1, keepdims=True)) / total
        logit_grad = dchosen * chosen * (1.0 - chosen)
        logit_full = jnp.sum(logit_grad[:, :, None] * pick, axis=1)
        router_back = jnp.dot(logit_full, router_w.astype(F32).T, precision=lax.Precision.HIGHEST)
        return (cot.astype(F32) + norm_pull(saved, gain, row_sum + router_back)).astype(BF16)

    forward_in = fwd_tokens[0]
    cotan_in = cotangent[0]
    saved = [saved_parts(t) for t in range(ticks)]
    saved_rows = lax.all_gather(
        jnp.concatenate([one[0] for one in saved], axis=0), "expert", axis_index_groups=column, tiled=True
    )
    normed = norm_rows(forward_in, gain).astype(BF16)
    rows_f, rows_c = dispatch(
        pack_rows(normed, fwd_spreads[0], 1),
        pack_rows(cotan_in, bwd_spreads[0], 1, saved[0][1]),
        first=(gate_r0,),
        then=((gate_r1, up_r), (saved_rows,)),
    )
    weights = (
        jnp.concatenate([w_gate[0], gate_r], axis=1),
        jnp.concatenate([w_up[0], up_r], axis=1),
        jnp.concatenate([w_down[0], down_r], axis=0),
    )
    for t in range(ticks):
        back_f, back_b = gather_back(
            run_kernel(forward_kernel, rows_f, weights, width, 3),
            run_kernel(
                functools.partial(backward_kernel, t, tokens, ticks),
                rows_c, (saved_rows,) + weights, width, 5, (part.reshape(1),),
            ),
        )
        fwd_result = finish_forward(t, forward_in, normed, back_f)
        bwd_result = finish_backward(t, cotan_in, saved[t][2], back_b)
        if t + 1 < ticks:
            forward_in = shift(fwd_result, "pipe", 1)
            cotan_in = shift(bwd_result, "pipe", -1)
            normed = norm_rows(forward_in, gain).astype(BF16)
            rows_f, rows_c = dispatch(
                pack_rows(normed, fwd_spreads[t + 1], 1),
                pack_rows(cotan_in, bwd_spreads[t + 1], 1, saved[t + 1][1]),
            )
    return (fwd_result[None], bwd_result[None])


def solution(mesh):
    return jax.shard_map(
        local,
        mesh=mesh,
        in_specs=(
            P("pipe", "expert", None),
            P(None, "pipe", "expert", None),
            P("pipe", "expert", None),
            P(None, "pipe", "expert", None),
            P(None, "pipe", "expert", None),
            P("pipe", None),
            P("pipe", None, None),
            P("pipe", None, "expert"),
            P("pipe", None, "expert"),
            P("pipe", "expert", None),
        ),
        out_specs=(P("pipe", "expert", None), P("pipe", "expert", None)),
        check_vma=False,
    )
```

```python
import functools

import jax
import jax.numpy as jnp
from jax import lax
from jax.experimental import pallas as pl
from jax.experimental.pallas import tpu as pltpu
from jax.sharding import PartitionSpec as P

BF16 = jnp.bfloat16
F32 = jnp.float32


def shift(block, axis, distance):
    size = lax.axis_size(axis)
    return lax.ppermute(block, axis, [((i - distance) % size, i) for i in range(size)])


def norm_rows(values, norm_gain):
    wide = values.astype(F32)
    scale = lax.rsqrt(jnp.mean(wide * wide, axis=-1, keepdims=True) + 1e-06)
    return wide * scale * norm_gain


def norm_pull(values, norm_gain, grad):
    wide = values.astype(F32)
    scale = lax.rsqrt(jnp.mean(wide * wide, axis=-1, keepdims=True) + 1e-06)
    scaled = grad * norm_gain
    inner = jnp.mean(scaled * wide, axis=-1, keepdims=True)
    return scale * (scaled - wide * (scale * scale) * inner)


def gate_values(normed, router_w, pick):
    logits = jnp.dot(normed, router_w, preferred_element_type=F32)
    sig_all = jax.nn.sigmoid(logits)
    chosen = jnp.sum(pick * sig_all[:, None, :], axis=-1)
    total = jnp.sum(chosen, axis=-1, keepdims=True)
    return chosen, total, chosen / total


def slot_places(routes, experts, cap):
    flat = routes.reshape(-1)
    hit = (flat[:, None] == jnp.arange(experts, dtype=jnp.int32)).astype(F32)
    count = flat.shape[0]
    earlier = (jnp.arange(count)[:, None] > jnp.arange(count)[None, :]).astype(F32)
    before = jnp.dot(earlier, hit, preferred_element_type=F32)
    slot = jnp.sum(before * hit, axis=1).astype(jnp.int32)
    place = hit[:, :, None] * (slot[:, None, None] == jnp.arange(cap, dtype=jnp.int32)).astype(F32)
    return place.reshape(routes.shape + (experts, cap))


def slab_sizes(width):
    return width // 2, width // 7


def pieces(rows, step):
    return jnp.concatenate([rows[:, i:i + step] for i in range(0, rows.shape[1], step)], axis=0)


def unpieces(stacked, count):
    tokens = stacked.shape[0] // count
    return jnp.concatenate([stacked[i * tokens:(i + 1) * tokens] for i in range(count)], axis=1)


def pack_rows(rows, spread, copies, scalars=None):
    tokens, width = rows.shape
    experts = spread.shape[1]
    half, piece = slab_sizes(width)
    eye2 = jnp.eye(2, dtype=F32)
    eye87 = jnp.eye(8, 7, dtype=F32)
    main = jnp.einsum("tes,hg->ehsgt", spread[:, :, :4], eye2).reshape(experts, 1, 8, 2 * tokens)
    tail = jnp.einsum("te,cd->ecdt", spread[:, :, 4], eye87).reshape(experts, 1, 8, 7 * tokens)
    main = jnp.broadcast_to(main, (experts, copies, 8, 2 * tokens)).reshape(-1, 2 * tokens)
    tail = jnp.broadcast_to(tail, (experts, copies, 8, 7 * tokens)).reshape(-1, 7 * tokens)
    out_main = jnp.dot(main.astype(BF16), pieces(rows, half), preferred_element_type=F32).astype(BF16)
    out_tail = jnp.dot(tail.astype(BF16), pieces(rows, piece), preferred_element_type=F32)
    if scalars is not None:
        extra = jnp.zeros((experts, 1, 8, piece), F32).at[:, 0, 7, :scalars.shape[1]].set(scalars)
        extra = jnp.broadcast_to(extra, (experts, copies, 8, piece)).reshape(-1, piece)
        out_tail = out_tail + extra
    slab = jnp.concatenate([out_main, out_tail.astype(BF16)], axis=1)
    return slab.reshape(experts * copies, 8, half + piece)


def combine_rows(slabs, weights):
    tokens, experts, cap = weights.shape
    copies = slabs.shape[0] // experts
    half = slabs.shape[2] * 7 // 9
    eye2 = jnp.eye(2, dtype=F32)
    eye78 = jnp.eye(7, 8, dtype=F32)
    flat = slabs.reshape(-1, slabs.shape[2])
    main = jnp.einsum("tes,gh->gtehs", weights[:, :, :4], eye2).reshape(2 * tokens, experts, 1, 8)
    tail = jnp.einsum("te,dc->dtec", weights[:, :, 4], eye78).reshape(7 * tokens, experts, 1, 8)
    main = jnp.broadcast_to(main, (2 * tokens, experts, copies, 8)).reshape(2 * tokens, -1)
    tail = jnp.broadcast_to(tail, (7 * tokens, experts, copies, 8)).reshape(7 * tokens, -1)
    sum_main = jnp.dot(main.astype(BF16), flat[:, :half], preferred_element_type=F32)
    sum_tail = jnp.dot(tail.astype(BF16), flat[:, half:], preferred_element_type=F32)
    return unpieces(sum_main, 2) + unpieces(sum_tail, 7)


def slot_scalars(slabs, count):
    half = slabs.shape[2] * 7 // 9
    return slabs[:, 7, half:half + count].astype(F32)


SOURCES = 16


def iota(shape, dim):
    return lax.broadcasted_iota(jnp.int32, shape, dim)


def one_hot(wanted, held):
    return jnp.where(wanted == held, 1.0, 0.0).astype(BF16)


def main_place(r):
    return (((r >> 2) & (SOURCES - 1)) << 3) | ((r >> 6) << 2) | (r & 3)


def tail_place(r):
    return ((r & (SOURCES - 1)) << 3) | (r >> 4)


def row_source(r):
    return jnp.where(r < 4 * SOURCES, r >> 2, r - 4 * SOURCES)


def row_slot(r):
    return jnp.where(r < 4 * SOURCES, r & 3, 4)


def dot(left, right, left_dim=1, right_dim=0):
    return lax.dot_general(
        left, right, (((left_dim,), (right_dim,)), ((), ())), preferred_element_type=F32
    )


def unpack(slabs, rows_ref):
    half, piece = slab_sizes(rows_ref.shape[1])
    count = 4 * SOURCES
    pick = one_hot(main_place(iota((2 * count, 8 * SOURCES), 0)), iota((2 * count, 8 * SOURCES), 1))
    main = dot(pick, slabs[:, :half]).astype(BF16)
    rows_ref[:count, :half] = main[:count]
    rows_ref[:count, half:] = main[count:]
    pick = one_hot(tail_place(iota((7 * SOURCES, 8 * SOURCES), 0)), iota((7 * SOURCES, 8 * SOURCES), 1))
    tail = dot(pick, slabs[:, half:]).astype(BF16)
    for i in range(7):
        rows_ref[count:, i * piece:(i + 1) * piece] = tail[i * SOURCES:(i + 1) * SOURCES]


def pack(rows, keep_ref, send_ref, scalars=None):
    half, piece = slab_sizes(rows.shape[1])
    count = 4 * SOURCES
    stacked = jnp.concatenate([rows[:count, :half], rows[:count, half:]], axis=0)
    pick = one_hot(main_place(iota((8 * SOURCES, 2 * count), 1)), iota((8 * SOURCES, 2 * count), 0))
    main = dot(pick, stacked).astype(BF16)
    stacked = jnp.concatenate([rows[count:, i * piece:(i + 1) * piece] for i in range(7)], axis=0)
    pick = one_hot(tail_place(iota((8 * SOURCES, 7 * SOURCES), 1)), iota((8 * SOURCES, 7 * SOURCES), 0))
    tail = dot(pick, stacked)
    mid = keep_ref.shape[0]
    keep_ref[:, :half] = main[:mid]
    send_ref[:, :half] = main[mid:]
    lanes = 0
    if scalars is not None:
        lanes = scalars.shape[1]
        first = (tail[:, :lanes] + scalars).astype(BF16)
        keep_ref[:, half:half + lanes] = first[:mid]
        send_ref[:, half:half + lanes] = first[mid:]
    tail = tail[:, lanes:].astype(BF16)
    keep_ref[:, half + lanes:] = tail[:mid]
    send_ref[:, half + lanes:] = tail[mid:]


def forward_kernel(near_ref, other_ref, gate_ref, up_ref, down_ref, keep_ref, send_ref, rows_ref):
    unpack(jnp.concatenate([near_ref[...], other_ref[...]], axis=0), rows_ref)
    rows = rows_ref[...]
    gate_pre = dot(rows, gate_ref[...])
    up_pre = dot(rows, up_ref[...])
    hidden = (gate_pre * jax.nn.sigmoid(gate_pre) * up_pre).astype(BF16)
    pack(dot(hidden, down_ref[...]).astype(BF16), keep_ref, send_ref)


def backward_kernel(
    tick, tokens, ticks, part_ref, saved_ref, near_ref, other_ref, gate_ref, up_ref, down_ref,
    keep_ref, send_ref, rows_ref,
):
    part = part_ref[0]
    slabs = jnp.concatenate([near_ref[...], other_ref[...]], axis=0)
    count = 5 * SOURCES
    half = slab_sizes(rows_ref.shape[1])[0]
    lanes = 128
    pick = one_hot((row_source(iota((count, 8 * SOURCES), 0)) << 3) | 7, iota((count, 8 * SOURCES), 1))
    scalars = dot(pick, slabs[:, half:half + lanes])
    slot = row_slot(iota((count, lanes), 0))
    lane = iota((count, lanes), 1)
    gb = jnp.sum(jnp.where(lane == slot, scalars, 0.0), axis=1, keepdims=True)
    token = jnp.sum(jnp.where(lane == slot + 5, scalars, 0.0), axis=1, keepdims=True).astype(jnp.int32)
    source = row_source(iota((count, 1), 0))
    away = (((source >> 2) & 1) << 1) | (source >> 3)
    depth_place = (away ^ part ^ (source & 2)) + ((source & 3) << 2)
    first = depth_place * (ticks * tokens) + tick * tokens
    wanted = jnp.where(token < 0, -1, first + token)
    pick = one_hot(wanted, iota((count, saved_ref.shape[0]), 1))
    rows = dot(pick, saved_ref[...]).astype(BF16)
    unpack(slabs, rows_ref)
    cot_hidden = dot(rows_ref[...], down_ref[...], 1, 1)
    gate_pre = dot(rows, gate_ref[...])
    up_pre = dot(rows, up_ref[...])
    gate_sig = jax.nn.sigmoid(gate_pre)
    gate_act = gate_pre * gate_sig
    hidden = (gate_act * up_pre).astype(BF16).astype(F32)
    dgate = jnp.sum(hidden * cot_hidden, axis=1, keepdims=True)
    hidden_grad = cot_hidden * gb
    gate_grad = (hidden_grad * up_pre * gate_sig * (1.0 + gate_pre * (1.0 - gate_sig))).astype(BF16)
    up_grad = (hidden_grad * gate_act).astype(BF16)
    grad = dot(gate_grad, gate_ref[...], 1, 1) + dot(up_grad, up_ref[...], 1, 1)
    high = dgate.astype(BF16).astype(F32)
    own = lane - part * 10
    both = jnp.where(own == slot, high, jnp.where(own == slot + 5, dgate - high, 0.0)).astype(BF16)
    place = one_hot((row_source(iota((8 * SOURCES, count), 1)) << 3) | 7, iota((8 * SOURCES, count), 0))
    pack(grad.astype(BF16), keep_ref, send_ref, dot(place, both))


def run_kernel(kernel, slabs, operands, width, products, scalars=()):
    near, other = [slab.reshape(-1, slab.shape[2]) for slab in slabs]
    vmem = pl.BlockSpec(memory_space=pltpu.VMEM)
    inputs = [*operands[:-3], near, other, *operands[-3:]]
    moved = sum(value.size * value.dtype.itemsize for value in inputs) + 2 * near.size * 2
    units = operands[-1].shape[0]
    out = pl.pallas_call(
        kernel,
        out_shape=[jax.ShapeDtypeStruct(near.shape, BF16)] * 2,
        in_specs=[pl.BlockSpec(memory_space=pltpu.SMEM)] * len(scalars) + [vmem] * len(inputs),
        out_specs=[vmem] * 2,
        scratch_shapes=[pltpu.VMEM((5 * SOURCES, width), BF16)],
        compiler_params=pltpu.CompilerParams(vmem_limit_bytes=16 << 20),
        cost_estimate=pl.CostEstimate(
            flops=2 * products * 5 * SOURCES * width * units, bytes_accessed=moved, transcendentals=0
        ),
    )(*scalars, *inputs)
    return [value.reshape(slabs[0].shape) for value in out]


def local(
    fwd_tokens,
    saved_tokens,
    cotangent,
    fwd_routes,
    bwd_routes,
    norm_gain,
    router,
    w_gate,
    w_up,
    w_down,
):
    gain = norm_gain[0]
    router_w = router[0]
    ticks = saved_tokens.shape[0]
    tokens, width = fwd_tokens.shape[1:]
    top = fwd_routes.shape[-1]
    experts = router_w.shape[1]
    cap = 5 * tokens * top // (4 * experts)
    ranks = lax.axis_size("expert")
    depth = ranks // 2
    copies = depth // experts
    partner = [(i, i ^ 1) for i in range(ranks)]
    turn = [e // 2 % 2 * 2 for e in range(experts)]
    far = [[x + 2 * ((p ^ turn[e]) + copies * e) for e in range(experts)] for p in range(copies) for x in range(2)]
    column = [[x + 2 * z for z in range(depth)] for x in range(2)]
    depth_place = lax.axis_index("expert") // 2
    part = (depth_place % copies) ^ (depth_place // copies // 2 % 2 * 2)

    def swap(slabs, groups):
        return lax.all_to_all(
            slabs, "expert", split_axis=0, concat_axis=0, axis_index_groups=groups, tiled=True
        )

    def after(value, *earlier):
        return lax.optimization_barrier((value,) + earlier)[0]

    def across(value, bit):
        return lax.ppermute(value, "expert", [(i, i ^ (2 * bit)) for i in range(ranks)])

    def spread_near(held):
        near = jnp.concatenate([held, across(held, 2)], axis=0)
        return near, across(near, 1)

    def add(left, right):
        return (left.astype(F32) + right.astype(F32)).astype(BF16)

    def gather_near(keep, send, then=()):
        parts = add(keep, across(after(send, *then), 1))
        count = parts.shape[0] // 2
        return add(parts[:count], across(parts[count:], 2))

    def dispatch(*slabs, first=(), then=()):
        held = after(swap(after(jnp.concatenate(slabs, axis=1), *first), far), *then)
        return [spread_near(held[:, 8 * i:8 * i + 8]) for i in range(len(slabs))]

    def gather_back(*slabs, then=((), ())):
        held = swap(jnp.concatenate([gather_near(*slab, then[i]) for i, slab in enumerate(slabs)], axis=1), far)
        return [held[:, 8 * i:8 * i + 8] for i in range(len(slabs))]

    half = w_gate.shape[1] // 2
    gate_r0 = lax.ppermute(w_gate[0, :half], "expert", partner)
    mixed = jnp.concatenate([w_gate[0, half:], w_up[0]], axis=0)
    mixed_r = lax.ppermute(after(mixed, gate_r0), "expert", partner)
    down_r = lax.ppermute(after(w_down[0], mixed_r), "expert", partner)
    gate_r = jnp.concatenate([gate_r0, mixed_r[:half]], axis=0)
    up_r = mixed_r[half:]

    expert_ids = jnp.arange(experts, dtype=jnp.int32)
    fwd_places = [slot_places(fwd_routes[t, 0], experts, cap) for t in range(ticks)]
    bwd_places = [slot_places(bwd_routes[t, 0], experts, cap) for t in range(ticks)]
    fwd_spreads = [jnp.sum(place, axis=1) for place in fwd_places]
    bwd_spreads = [jnp.sum(place, axis=1) for place in bwd_places]

    def saved_parts(t):
        saved = saved_tokens[t, 0]
        saved_norm = norm_rows(saved, gain).astype(BF16)
        pick = (bwd_routes[t, 0][..., None] == expert_ids).astype(F32)
        chosen, total, share = gate_values(saved_norm, router_w, pick)
        gb = share.astype(BF16).astype(F32)
        slot_gb = jnp.sum(bwd_places[t] * gb[:, :, None, None], axis=(0, 1))
        ids = jnp.arange(1, tokens + 1, dtype=F32)
        slot_token = jnp.sum(bwd_spreads[t] * ids[:, None, None], axis=0) - 1.0
        scalars = jnp.concatenate([slot_gb, slot_token], axis=1)
        return saved_norm, scalars, (saved, pick, chosen, total, share)

    def finish_forward(t, tokens_in, normed, back):
        pick = (fwd_routes[t, 0][..., None] == expert_ids).astype(F32)
        _, _, share = gate_values(normed, router_w, pick)
        gb = share.astype(BF16).astype(F32)
        weights = jnp.sum(fwd_places[t] * gb[:, :, None, None], axis=1)
        return (tokens_in.astype(F32) + combine_rows(back, weights)).astype(BF16)

    def finish_backward(t, cot, parts, back):
        saved, pick, chosen, total, share = parts
        row_sum = combine_rows(back, bwd_spreads[t])
        slot_dgate = slot_scalars(back, copies * 2 * cap).reshape(experts, copies * 2, cap).sum(axis=1)
        dgate = jnp.sum(bwd_places[t] * slot_dgate, axis=(2, 3))
        dchosen = (dgate - jnp.sum(share * dgate, axis=-1, keepdims=True)) / total
        logit_grad = dchosen * chosen * (1.0 - chosen)
        logit_full = jnp.sum(logit_grad[:, :, None] * pick, axis=1)
        router_back = jnp.dot(logit_full, router_w.astype(F32).T, precision=lax.Precision.HIGHEST)
        return (cot.astype(F32) + norm_pull(saved, gain, row_sum + router_back)).astype(BF16)

    forward_in = fwd_tokens[0]
    cotan_in = cotangent[0]
    saved = [saved_parts(t) for t in range(ticks)]
    saved_rows = lax.all_gather(
        jnp.concatenate([one[0] for one in saved], axis=0), "expert", axis_index_groups=column, tiled=True
    )
    normed = norm_rows(forward_in, gain).astype(BF16)
    rows_f, rows_c = dispatch(
        pack_rows(normed, fwd_spreads[0], 1),
        pack_rows(cotan_in, bwd_spreads[0], 1, saved[0][1]),
        first=(gate_r0,),
        then=(mixed_r,),
    )
    weights = (
        jnp.concatenate([w_gate[0], gate_r], axis=1),
        jnp.concatenate([w_up[0], up_r], axis=1),
        jnp.concatenate([w_down[0], down_r], axis=0),
    )
    for t in range(ticks):
        back_f, back_b = gather_back(
            run_kernel(forward_kernel, rows_f, weights, width, 3),
            run_kernel(
                functools.partial(backward_kernel, t, tokens, ticks),
                rows_c, (saved_rows,) + weights, width, 5, (part.reshape(1),),
            ),
            then=((saved_rows,) if t == 0 else (), ()),
        )
        fwd_result = finish_forward(t, forward_in, normed, back_f)
        bwd_result = finish_backward(t, cotan_in, saved[t][2], back_b)
        if t + 1 < ticks:
            fwd_result, bwd_result = lax.optimization_barrier((fwd_result, bwd_result))
            forward_in = shift(fwd_result, "pipe", 1)
            cotan_in = shift(bwd_result, "pipe", -1)
            normed = norm_rows(forward_in, gain).astype(BF16)
            rows_f, rows_c = dispatch(
                pack_rows(normed, fwd_spreads[t + 1], 1),
                pack_rows(cotan_in, bwd_spreads[t + 1], 1, saved[t + 1][1]),
            )
    return (fwd_result[None], bwd_result[None])


def solution(mesh):
    return jax.shard_map(
        local,
        mesh=mesh,
        in_specs=(
            P("pipe", "expert", None),
            P(None, "pipe", "expert", None),
            P("pipe", "expert", None),
            P(None, "pipe", "expert", None),
            P(None, "pipe", "expert", None),
            P("pipe", None),
            P("pipe", None, None),
            P("pipe", None, "expert"),
            P("pipe", None, "expert"),
            P("pipe", "expert", None),
        ),
        out_specs=(P("pipe", "expert", None), P("pipe", "expert", None)),
        check_vma=False,
    )
```

```python
import functools

import jax
import jax.numpy as jnp
from jax import lax
from jax.experimental import pallas as pl
from jax.experimental.pallas import tpu as pltpu
from jax.sharding import PartitionSpec as P

BF16 = jnp.bfloat16
F32 = jnp.float32


def shift(block, axis, distance):
    size = lax.axis_size(axis)
    return lax.ppermute(block, axis, [((i - distance) % size, i) for i in range(size)])


def norm_rows(values, norm_gain):
    wide = values.astype(F32)
    scale = lax.rsqrt(jnp.mean(wide * wide, axis=-1, keepdims=True) + 1e-06)
    return wide * scale * norm_gain


def norm_pull(values, norm_gain, grad):
    wide = values.astype(F32)
    scale = lax.rsqrt(jnp.mean(wide * wide, axis=-1, keepdims=True) + 1e-06)
    scaled = grad * norm_gain
    inner = jnp.mean(scaled * wide, axis=-1, keepdims=True)
    return scale * (scaled - wide * (scale * scale) * inner)


def gate_values(normed, router_w, pick):
    logits = jnp.dot(normed, router_w, preferred_element_type=F32)
    sig_all = jax.nn.sigmoid(logits)
    chosen = jnp.sum(pick * sig_all[:, None, :], axis=-1)
    total = jnp.sum(chosen, axis=-1, keepdims=True)
    return chosen, total, chosen / total


def slot_places(routes, experts, cap):
    flat = routes.reshape(-1)
    hit = (flat[:, None] == jnp.arange(experts, dtype=jnp.int32)).astype(F32)
    count = flat.shape[0]
    earlier = (jnp.arange(count)[:, None] > jnp.arange(count)[None, :]).astype(F32)
    before = jnp.dot(earlier, hit, preferred_element_type=F32)
    slot = jnp.sum(before * hit, axis=1).astype(jnp.int32)
    place = hit[:, :, None] * (slot[:, None, None] == jnp.arange(cap, dtype=jnp.int32)).astype(F32)
    return place.reshape(routes.shape + (experts, cap))


def slab_sizes(width):
    return width // 2, width // 7


def pieces(rows, step):
    return jnp.concatenate([rows[:, i:i + step] for i in range(0, rows.shape[1], step)], axis=0)


def unpieces(stacked, count):
    tokens = stacked.shape[0] // count
    return jnp.concatenate([stacked[i * tokens:(i + 1) * tokens] for i in range(count)], axis=1)


def pack_rows(rows, spread, copies, scalars=None):
    tokens, width = rows.shape
    experts = spread.shape[1]
    half, piece = slab_sizes(width)
    eye2 = jnp.eye(2, dtype=F32)
    eye87 = jnp.eye(8, 7, dtype=F32)
    main = jnp.einsum("tes,hg->ehsgt", spread[:, :, :4], eye2).reshape(experts, 1, 8, 2 * tokens)
    tail = jnp.einsum("te,cd->ecdt", spread[:, :, 4], eye87).reshape(experts, 1, 8, 7 * tokens)
    main = jnp.broadcast_to(main, (experts, copies, 8, 2 * tokens)).reshape(-1, 2 * tokens)
    tail = jnp.broadcast_to(tail, (experts, copies, 8, 7 * tokens)).reshape(-1, 7 * tokens)
    out_main = jnp.dot(main.astype(BF16), pieces(rows, half), preferred_element_type=F32).astype(BF16)
    out_tail = jnp.dot(tail.astype(BF16), pieces(rows, piece), preferred_element_type=F32)
    if scalars is not None:
        extra = jnp.zeros((experts, 1, 8, piece), F32).at[:, 0, 7, :scalars.shape[1]].set(scalars)
        extra = jnp.broadcast_to(extra, (experts, copies, 8, piece)).reshape(-1, piece)
        out_tail = out_tail + extra
    slab = jnp.concatenate([out_main, out_tail.astype(BF16)], axis=1)
    return slab.reshape(experts * copies, 8, half + piece)


def combine_rows(slabs, weights):
    tokens, experts, cap = weights.shape
    copies = slabs.shape[0] // experts
    half = slabs.shape[2] * 7 // 9
    eye2 = jnp.eye(2, dtype=F32)
    eye78 = jnp.eye(7, 8, dtype=F32)
    flat = slabs.reshape(-1, slabs.shape[2])
    main = jnp.einsum("tes,gh->gtehs", weights[:, :, :4], eye2).reshape(2 * tokens, experts, 1, 8)
    tail = jnp.einsum("te,dc->dtec", weights[:, :, 4], eye78).reshape(7 * tokens, experts, 1, 8)
    main = jnp.broadcast_to(main, (2 * tokens, experts, copies, 8)).reshape(2 * tokens, -1)
    tail = jnp.broadcast_to(tail, (7 * tokens, experts, copies, 8)).reshape(7 * tokens, -1)
    sum_main = jnp.dot(main.astype(BF16), flat[:, :half], preferred_element_type=F32)
    sum_tail = jnp.dot(tail.astype(BF16), flat[:, half:], preferred_element_type=F32)
    return unpieces(sum_main, 2) + unpieces(sum_tail, 7)


def slot_scalars(slabs, count):
    half = slabs.shape[2] * 7 // 9
    return slabs[:, 7, half:half + count].astype(F32)


SOURCES = 16


def iota(shape, dim):
    return lax.broadcasted_iota(jnp.int32, shape, dim)


def one_hot(wanted, held):
    return jnp.where(wanted == held, 1.0, 0.0).astype(BF16)


def main_place(r):
    return (((r >> 2) & (SOURCES - 1)) << 3) | ((r >> 6) << 2) | (r & 3)


def tail_place(r):
    return ((r & (SOURCES - 1)) << 3) | (r >> 4)


def row_source(r):
    return jnp.where(r < 4 * SOURCES, r >> 2, r - 4 * SOURCES)


def row_slot(r):
    return jnp.where(r < 4 * SOURCES, r & 3, 4)


def dot(left, right, left_dim=1, right_dim=0):
    return lax.dot_general(
        left, right, (((left_dim,), (right_dim,)), ((), ())), preferred_element_type=F32
    )


def unpack(slabs, rows_ref):
    half, piece = slab_sizes(rows_ref.shape[1])
    count = 4 * SOURCES
    pick = one_hot(main_place(iota((2 * count, 8 * SOURCES), 0)), iota((2 * count, 8 * SOURCES), 1))
    main = dot(pick, slabs[:, :half]).astype(BF16)
    rows_ref[:count, :half] = main[:count]
    rows_ref[:count, half:] = main[count:]
    pick = one_hot(tail_place(iota((7 * SOURCES, 8 * SOURCES), 0)), iota((7 * SOURCES, 8 * SOURCES), 1))
    tail = dot(pick, slabs[:, half:]).astype(BF16)
    for i in range(7):
        rows_ref[count:, i * piece:(i + 1) * piece] = tail[i * SOURCES:(i + 1) * SOURCES]


def pack(rows, keep_ref, send_ref, scalars=None):
    half, piece = slab_sizes(rows.shape[1])
    count = 4 * SOURCES
    stacked = jnp.concatenate([rows[:count, :half], rows[:count, half:]], axis=0)
    pick = one_hot(main_place(iota((8 * SOURCES, 2 * count), 1)), iota((8 * SOURCES, 2 * count), 0))
    main = dot(pick, stacked).astype(BF16)
    stacked = jnp.concatenate([rows[count:, i * piece:(i + 1) * piece] for i in range(7)], axis=0)
    pick = one_hot(tail_place(iota((8 * SOURCES, 7 * SOURCES), 1)), iota((8 * SOURCES, 7 * SOURCES), 0))
    tail = dot(pick, stacked)
    mid = keep_ref.shape[0]
    keep_ref[:, :half] = main[:mid]
    send_ref[:, :half] = main[mid:]
    lanes = 0
    if scalars is not None:
        lanes = scalars.shape[1]
        first = (tail[:, :lanes] + scalars).astype(BF16)
        keep_ref[:, half:half + lanes] = first[:mid]
        send_ref[:, half:half + lanes] = first[mid:]
    tail = tail[:, lanes:].astype(BF16)
    keep_ref[:, half + lanes:] = tail[:mid]
    send_ref[:, half + lanes:] = tail[mid:]


def forward_kernel(near_ref, other_ref, gate_ref, up_ref, down_ref, keep_ref, send_ref, rows_ref):
    unpack(jnp.concatenate([near_ref[...], other_ref[...]], axis=0), rows_ref)
    rows = rows_ref[...]
    gate_pre = dot(rows, gate_ref[...])
    up_pre = dot(rows, up_ref[...])
    hidden = (gate_pre * jax.nn.sigmoid(gate_pre) * up_pre).astype(BF16)
    pack(dot(hidden, down_ref[...]).astype(BF16), keep_ref, send_ref)


def backward_kernel(
    tick, tokens, ticks, part_ref, saved_ref, near_ref, other_ref, gate_ref, up_ref, down_ref,
    keep_ref, send_ref, rows_ref,
):
    part = part_ref[0]
    slabs = jnp.concatenate([near_ref[...], other_ref[...]], axis=0)
    count = 5 * SOURCES
    half = slab_sizes(rows_ref.shape[1])[0]
    lanes = 128
    pick = one_hot((row_source(iota((count, 8 * SOURCES), 0)) << 3) | 7, iota((count, 8 * SOURCES), 1))
    scalars = dot(pick, slabs[:, half:half + lanes])
    slot = row_slot(iota((count, lanes), 0))
    lane = iota((count, lanes), 1)
    gb = jnp.sum(jnp.where(lane == slot, scalars, 0.0), axis=1, keepdims=True)
    token = jnp.sum(jnp.where(lane == slot + 5, scalars, 0.0), axis=1, keepdims=True).astype(jnp.int32)
    source = row_source(iota((count, 1), 0))
    away = (((source >> 2) & 1) << 1) | (source >> 3)
    depth_place = (away ^ part ^ (source & 2)) + ((source & 3) << 2)
    first = depth_place * (ticks * tokens) + tick * tokens
    wanted = jnp.where(token < 0, -1, first + token)
    pick = one_hot(wanted, iota((count, saved_ref.shape[0]), 1))
    rows = dot(pick, saved_ref[...]).astype(BF16)
    unpack(slabs, rows_ref)
    cot_hidden = dot(rows_ref[...], down_ref[...], 1, 1)
    gate_pre = dot(rows, gate_ref[...])
    up_pre = dot(rows, up_ref[...])
    gate_sig = jax.nn.sigmoid(gate_pre)
    gate_act = gate_pre * gate_sig
    hidden = (gate_act * up_pre).astype(BF16).astype(F32)
    dgate = jnp.sum(hidden * cot_hidden, axis=1, keepdims=True)
    hidden_grad = cot_hidden * gb
    gate_grad = (hidden_grad * up_pre * gate_sig * (1.0 + gate_pre * (1.0 - gate_sig))).astype(BF16)
    up_grad = (hidden_grad * gate_act).astype(BF16)
    grad = dot(gate_grad, gate_ref[...], 1, 1) + dot(up_grad, up_ref[...], 1, 1)
    high = dgate.astype(BF16).astype(F32)
    own = lane - part * 10
    both = jnp.where(own == slot, high, jnp.where(own == slot + 5, dgate - high, 0.0)).astype(BF16)
    place = one_hot((row_source(iota((8 * SOURCES, count), 1)) << 3) | 7, iota((8 * SOURCES, count), 0))
    pack(grad.astype(BF16), keep_ref, send_ref, dot(place, both))


def run_kernel(kernel, slabs, operands, width, products, scalars=()):
    near, other = [slab.reshape(-1, slab.shape[2]) for slab in slabs]
    vmem = pl.BlockSpec(memory_space=pltpu.VMEM)
    inputs = [*operands[:-3], near, other, *operands[-3:]]
    moved = sum(value.size * value.dtype.itemsize for value in inputs) + 2 * near.size * 2
    units = operands[-1].shape[0]
    out = pl.pallas_call(
        kernel,
        out_shape=[jax.ShapeDtypeStruct(near.shape, BF16)] * 2,
        in_specs=[pl.BlockSpec(memory_space=pltpu.SMEM)] * len(scalars) + [vmem] * len(inputs),
        out_specs=[vmem] * 2,
        scratch_shapes=[pltpu.VMEM((5 * SOURCES, width), BF16)],
        compiler_params=pltpu.CompilerParams(vmem_limit_bytes=16 << 20),
        cost_estimate=pl.CostEstimate(
            flops=2 * products * 5 * SOURCES * width * units, bytes_accessed=moved, transcendentals=0
        ),
    )(*scalars, *inputs)
    return [value.reshape(slabs[0].shape) for value in out]


def local(
    fwd_tokens,
    saved_tokens,
    cotangent,
    fwd_routes,
    bwd_routes,
    norm_gain,
    router,
    w_gate,
    w_up,
    w_down,
):
    gain = norm_gain[0]
    router_w = router[0]
    ticks = saved_tokens.shape[0]
    tokens, width = fwd_tokens.shape[1:]
    top = fwd_routes.shape[-1]
    experts = router_w.shape[1]
    cap = 5 * tokens * top // (4 * experts)
    ranks = lax.axis_size("expert")
    depth = ranks // 2
    copies = depth // experts
    partner = [(i, i ^ 1) for i in range(ranks)]
    turn = [e // 2 % 2 * 2 for e in range(experts)]
    far = [[x + 2 * ((p ^ turn[e]) + copies * e) for e in range(experts)] for p in range(copies) for x in range(2)]
    column = [[x + 2 * z for z in range(depth)] for x in range(2)]
    depth_place = lax.axis_index("expert") // 2
    part = (depth_place % copies) ^ (depth_place // copies // 2 % 2 * 2)

    def swap(slabs, groups):
        return lax.all_to_all(
            slabs, "expert", split_axis=0, concat_axis=0, axis_index_groups=groups, tiled=True
        )

    def after(value, *earlier):
        return lax.optimization_barrier((value,) + earlier)[0]

    def across(value, bit):
        return lax.ppermute(value, "expert", [(i, i ^ (2 * bit)) for i in range(ranks)])

    def spread_near(held):
        near = jnp.concatenate([held, across(held, 2)], axis=0)
        return near, across(near, 1)

    def add(left, right):
        return (left.astype(F32) + right.astype(F32)).astype(BF16)

    def gather_near(keep, send, then=()):
        parts = add(keep, across(after(send, *then), 1))
        count = parts.shape[0] // 2
        return add(parts[:count], across(parts[count:], 2))

    def dispatch(*slabs, first=(), then=(), turns=False):
        held = after(swap(after(jnp.concatenate(slabs, axis=1), *first), far), *then)
        spread = []
        for i in range(len(slabs)):
            ahead = [spread[-1][0]] if turns and spread else []
            spread.append(spread_near(after(held[:, 8 * i:8 * i + 8], *ahead)))
        return spread

    def gather_back(*slabs, then=((), ())):
        held = swap(jnp.concatenate([gather_near(*slab, then[i]) for i, slab in enumerate(slabs)], axis=1), far)
        return [held[:, 8 * i:8 * i + 8] for i in range(len(slabs))]

    half = w_gate.shape[1] // 2
    gate_r0 = lax.ppermute(w_gate[0, :half], "expert", partner)
    mixed = jnp.concatenate([w_gate[0, half:], w_up[0]], axis=0)
    mixed_r = lax.ppermute(after(mixed, gate_r0), "expert", partner)
    down_r = lax.ppermute(after(w_down[0], mixed_r), "expert", partner)
    gate_r = jnp.concatenate([gate_r0, mixed_r[:half]], axis=0)
    up_r = mixed_r[half:]

    expert_ids = jnp.arange(experts, dtype=jnp.int32)
    fwd_places = [slot_places(fwd_routes[t, 0], experts, cap) for t in range(ticks)]
    bwd_places = [slot_places(bwd_routes[t, 0], experts, cap) for t in range(ticks)]
    fwd_spreads = [jnp.sum(place, axis=1) for place in fwd_places]
    bwd_spreads = [jnp.sum(place, axis=1) for place in bwd_places]

    def saved_parts(t):
        saved = saved_tokens[t, 0]
        saved_norm = norm_rows(saved, gain).astype(BF16)
        pick = (bwd_routes[t, 0][..., None] == expert_ids).astype(F32)
        chosen, total, share = gate_values(saved_norm, router_w, pick)
        gb = share.astype(BF16).astype(F32)
        slot_gb = jnp.sum(bwd_places[t] * gb[:, :, None, None], axis=(0, 1))
        ids = jnp.arange(1, tokens + 1, dtype=F32)
        slot_token = jnp.sum(bwd_spreads[t] * ids[:, None, None], axis=0) - 1.0
        scalars = jnp.concatenate([slot_gb, slot_token], axis=1)
        return saved_norm, scalars, (saved, pick, chosen, total, share)

    def finish_forward(t, tokens_in, normed, back):
        pick = (fwd_routes[t, 0][..., None] == expert_ids).astype(F32)
        _, _, share = gate_values(normed, router_w, pick)
        gb = share.astype(BF16).astype(F32)
        weights = jnp.sum(fwd_places[t] * gb[:, :, None, None], axis=1)
        return (tokens_in.astype(F32) + combine_rows(back, weights)).astype(BF16)

    def finish_backward(t, cot, parts, back):
        saved, pick, chosen, total, share = parts
        row_sum = combine_rows(back, bwd_spreads[t])
        slot_dgate = slot_scalars(back, copies * 2 * cap).reshape(experts, copies * 2, cap).sum(axis=1)
        dgate = jnp.sum(bwd_places[t] * slot_dgate, axis=(2, 3))
        dchosen = (dgate - jnp.sum(share * dgate, axis=-1, keepdims=True)) / total
        logit_grad = dchosen * chosen * (1.0 - chosen)
        logit_full = jnp.sum(logit_grad[:, :, None] * pick, axis=1)
        router_back = jnp.dot(logit_full, router_w.astype(F32).T, precision=lax.Precision.HIGHEST)
        return (cot.astype(F32) + norm_pull(saved, gain, row_sum + router_back)).astype(BF16)

    forward_in = fwd_tokens[0]
    cotan_in = cotangent[0]
    saved = [saved_parts(t) for t in range(ticks)]
    saved_rows = lax.all_gather(
        jnp.concatenate([one[0] for one in saved], axis=0), "expert", axis_index_groups=column, tiled=True
    )
    normed = norm_rows(forward_in, gain).astype(BF16)
    rows_f, rows_c = dispatch(
        pack_rows(normed, fwd_spreads[0], 1),
        pack_rows(cotan_in, bwd_spreads[0], 1, saved[0][1]),
        first=(gate_r0,),
        then=(mixed_r,),
    )
    weights = (
        jnp.concatenate([w_gate[0], gate_r], axis=1),
        jnp.concatenate([w_up[0], up_r], axis=1),
        jnp.concatenate([w_down[0], down_r], axis=0),
    )
    for t in range(ticks):
        back_f, back_b = gather_back(
            run_kernel(forward_kernel, rows_f, weights, width, 3),
            run_kernel(
                functools.partial(backward_kernel, t, tokens, ticks),
                rows_c, (saved_rows,) + weights, width, 5, (part.reshape(1),),
            ),
            then=((saved_rows,) if t == 0 else (), ()),
        )
        fwd_result = finish_forward(t, forward_in, normed, back_f)
        bwd_result = finish_backward(t, cotan_in, saved[t][2], back_b)
        if t + 1 < ticks:
            fwd_result, bwd_result = lax.optimization_barrier((fwd_result, bwd_result))
            forward_in = shift(fwd_result, "pipe", 1)
            cotan_in = shift(bwd_result, "pipe", -1)
            normed = norm_rows(forward_in, gain).astype(BF16)
            rows_f, rows_c = dispatch(
                pack_rows(normed, fwd_spreads[t + 1], 1),
                pack_rows(cotan_in, bwd_spreads[t + 1], 1, saved[t + 1][1]),
                turns=True,
            )
    return (fwd_result[None], bwd_result[None])


def solution(mesh):
    return jax.shard_map(
        local,
        mesh=mesh,
        in_specs=(
            P("pipe", "expert", None),
            P(None, "pipe", "expert", None),
            P("pipe", "expert", None),
            P(None, "pipe", "expert", None),
            P(None, "pipe", "expert", None),
            P("pipe", None),
            P("pipe", None, None),
            P("pipe", None, "expert"),
            P("pipe", None, "expert"),
            P("pipe", "expert", None),
        ),
        out_specs=(P("pipe", "expert", None), P("pipe", "expert", None)),
        check_vma=False,
    )
```
